256 devices in a mesh: ctx: 16 (over x_lo, z), head: 16 (over x_hi, y, core).
Axes of the slice: x: 4 (x_hi: 2, x_lo: 2; x = x_hi * 2 + x_lo), y: 4, z: 8, core: 2. Of those that a mesh axis runs over, the one named last changes fastest.
Arguments:
- queries: bfloat16 [6144, 4, 4096], P(('ctx', 'head')), may hold values from -84 to 84
- key_states: bfloat16 [6144, 4, 4096], P(('ctx', 'head')), may hold values from -4 to 4
- value_states: bfloat16 [6144, 4, 4096], P(('ctx', 'head')), may hold values from -6 to 6
- out_grad: bfloat16 [6144, 4096], P(('ctx', 'head')), may hold values from -6 to 6
- offsets: int32 [32], replicated, may hold values from 0 to 3
- block_mask: int32 [12, 12], replicated, may hold values from 0 to 1, as said below
Outputs:
- attended: bfloat16 [6144, 4096], P(('ctx', 'head'))
- query_grad: bfloat16 [6144, 4096], P(('ctx', 'head'))
- key_grad: bfloat16 [6144, 4096], P(('ctx', 'head'))
- value_grad: bfloat16 [6144, 4096], P(('ctx', 'head'))
The draws below stay inside these ranges and needn't reach their ends.
Inputs may be any that keep to these rules, and one draw needn't show every extreme that they name: block_mask is 1 on its diagonal and 0 above it.
All inputs are finite; a program needn't handle non-finite values.
Results may differ from the reference program's by a relative error of at most 0.015.
Values may be sent and summed in bfloat16 or wider, within the bound.
A program may use at most 128 MiB of HBM per device.

```python
import jax
import jax.numpy as jnp
from jax import lax

HEADS = 32
HD = 128
RES = 4
BLK = 512
WIDTH = 4096
NK = 6144
NB = 12


def shared_keys(key):
    normal_base = jax.random.normal(key, (NK, RES, HEADS * HD), jnp.float32)
    return jnp.clip(normal_base, -4.0, 4.0)


def draw_key_states(key, part):
    key_rows = shared_keys(key)
    return key_rows.astype(jnp.bfloat16)


def draw_queries(key, part):
    key_rows = shared_keys(key)
    key = jax.random.fold_in(key, 7)
    result = 3.5 * jnp.clip(jax.random.normal(key, key_rows.shape, jnp.float32), -4.0, 4.0)
    return result.astype(jnp.bfloat16)


def draw_block_mask(key, part):
    key = jax.random.fold_in(key, 5)
    coins = jax.random.randint(key, (NB, NB), 0, 2)
    row_index = jnp.arange(NB)[:, None]
    col_index = jnp.arange(NB)[None, :]
    return jnp.where(row_index == col_index, 1, jnp.where(col_index < row_index, coins, 0)).astype(jnp.int32)


def set_ends(entries, rng, smallest, high):
    longest = entries.shape.index(max(entries.shape))
    spots = []
    for shift in (0, 1):
        where = [jax.random.randint(jax.random.fold_in(rng, axis), (), 0, length) for axis, length in enumerate(entries.shape)]
        where[longest] = (where[longest] + shift) % entries.shape[longest]
        spots.append(tuple(where))
    return entries.at[spots[0]].set(smallest).at[spots[1]].set(high)


def levels(key, dims, pieces, low, largest):
    loudness = 1.0
    for axis_at, blocks in pieces:
        draws = jax.random.uniform(jax.random.fold_in(jax.random.fold_in(key, 6), axis_at), (blocks,), jnp.float32, low / len(pieces), largest / len(pieces))
        loudness = loudness * jnp.repeat(jnp.exp(draws), dims[axis_at] // blocks).reshape((-1,) + (1,) * (len(dims) - 1 - axis_at))
    return loudness


def centred(rng, dims, width, reach, cuts=(), held_as=jnp.bfloat16):
    loudness = levels(rng, dims, cuts, -0.22, 0.18) if cuts else 1.0
    values = jax.random.normal(rng, dims, jnp.float32) * width * loudness
    return jnp.minimum(jnp.maximum(values, -reach), reach).astype(held_as)


def setup_inputs(seed: int = 0) -> dict:
    arg_keys = jax.random.split(jax.random.key(seed), 7)
    queries = draw_queries(jax.random.fold_in(arg_keys[6], 71), 0)
    key_states = draw_key_states(jax.random.fold_in(arg_keys[6], 71), 0)
    value_states = centred(arg_keys[2], (NK, RES, WIDTH), 1.0, 6.0, ((0, 256),))
    out_grad = centred(arg_keys[3], (NK, WIDTH), 1.0, 6.0, ((0, 256),))
    offsets = set_ends(jax.random.randint(arg_keys[4], (HEADS,), 0, RES), jax.random.fold_in(arg_keys[4], 1), 0, RES - 1).astype(jnp.int32)
    block_mask = draw_block_mask(jax.random.fold_in(arg_keys[6], 71), 0)
    return {"queries": queries, "key_states": key_states, "value_states": value_states, "out_grad": out_grad, "offsets": offsets, "block_mask": block_mask}


def select_heads(states, offsets):
    split_view = states.reshape(NK, RES, HEADS, HD)
    chosen = jnp.arange(RES, dtype=jnp.int32)[:, None] == offsets[None, :]
    picked = jnp.sum(jnp.where(chosen[None, :, :, None], split_view, jnp.zeros_like(split_view)), axis=1)
    return jnp.transpose(picked, (1, 0, 2))


def allowed_matrix(block_mask):
    row_index = jnp.arange(NK, dtype=jnp.int32)
    one_hot = (row_index[:, None] // BLK == jnp.arange(NB, dtype=jnp.int32)[None, :]).astype(jnp.float32)
    listed = jnp.dot(jnp.dot(one_hot, block_mask.astype(jnp.float32)), one_hot.T) > 0.5
    return listed & (row_index[None, :] <= row_index[:, None])


def head_pass(allowed, query_rows, key_rows, value_rows, grad_rows):
    scale_factor = HD ** -0.5
    scores = jnp.dot(query_rows, key_rows.T, preferred_element_type=jnp.float32) * scale_factor
    row_max = jnp.max(jnp.where(allowed, scores, -jnp.inf), axis=1, keepdims=True)
    row_sum = jnp.sum(jnp.where(allowed, jnp.exp(scores - row_max), 0.0), axis=1, keepdims=True)
    log_sum = row_max + jnp.log(row_sum)
    prob_bf = jnp.where(allowed, jnp.exp(scores - log_sum), 0.0).astype(jnp.bfloat16)
    attended = jnp.dot(prob_bf, value_rows, preferred_element_type=jnp.float32).astype(jnp.bfloat16)
    row_dot = jnp.sum(grad_rows.astype(jnp.float32) * attended.astype(jnp.float32), axis=1, keepdims=True)
    prob_grad = jnp.dot(grad_rows, value_rows.T, preferred_element_type=jnp.float32)
    score_grad = (prob_bf.astype(jnp.float32) * (prob_grad - row_dot) * scale_factor).astype(jnp.bfloat16)
    query_grad = jnp.dot(score_grad, key_rows, preferred_element_type=jnp.float32).astype(jnp.bfloat16)
    key_grad = jnp.dot(score_grad.T, query_rows, preferred_element_type=jnp.float32).astype(jnp.bfloat16)
    value_grad = jnp.dot(prob_bf.T, grad_rows, preferred_element_type=jnp.float32).astype(jnp.bfloat16)
    return attended, query_grad, key_grad, value_grad


def reference(queries, key_states, value_states, out_grad, offsets, block_mask):
    allowed = allowed_matrix(block_mask)
    query_heads = select_heads(queries, offsets)
    key_heads = select_heads(key_states, offsets)
    value_heads = select_heads(value_states, offsets)
    grad_heads = jnp.transpose(out_grad.reshape(NK, HEADS, HD), (1, 0, 2))
    results = lax.map(lambda packed: head_pass(allowed, packed[0], packed[1], packed[2], packed[3]),
                      (query_heads, key_heads, value_heads, grad_heads))
    merged = [jnp.transpose(result, (1, 0, 2)).reshape(NK, HEADS * HD) for result in results]
    return merged[0], merged[1], merged[2], merged[3]
```

```python
import jax, jax.numpy as jnp
from jax.sharding import PartitionSpec as P
from jax import lax
from jax.experimental import pallas as pl
from jax.experimental.pallas import tpu as pltpu
BF=jnp.bfloat16; F32=jnp.float32
NB=12; BLK=512; TQ=256; HD=128
SCALE=HD**-0.5
C2=SCALE*1.4426950408889634

def dot(a,b):
    return jnp.dot(a,b,preferred_element_type=F32)

def attend_kernel(where_ref, mask_ref, kv_hbm, qg_ref, dkv_hbm, og_ref,
                  k_vm, v_vm, kt, vt, p_sc, m_sc, dk_acc, dv_acc, ot_acc, dqt_acc, live, sem):
    grp=where_ref[0]; core=where_ref[1]
    loads=[pltpu.make_async_copy(kv_hbm.at[:,i],r.reshape(256,3,8,HD),sem.at[i]) for i,r in enumerate((k_vm,v_vm))]
    for l in loads: l.start()
    @pl.loop(0,NB)
    def _(j):
        z=jnp.zeros((BLK,HD),F32)
        rows=pl.ds(pl.multiple_of(j*BLK,BLK),BLK)
        dk_acc[rows]=z; dv_acc[rows]=z
    for l in loads: l.wait()
    def blk(ref,j):
        return ref[pl.ds(pl.multiple_of(j*64,64),64)].reshape(BLK,HD)
    @pl.loop(0,NB)
    def _(j):
        kt[j]=blk(k_vm,j).T
        vt[j]=blk(v_vm,j).T
    def tile(t,_):
        bm=grp
        b=t*4+bm+(t%2)*(3-2*bm)
        half=(core+t)%2
        q=qg_ref[t,0].reshape(TQ,HD); g=qg_ref[t,1].reshape(TQ,HD)
        qt=q.T; gt=g.T
        def count(j,n):
            live[n]=j
            return n+mask_ref[b,j]
        n_live=lax.fori_loop(0,b,count,0)
        def fwd(j,slot,diag,m,l):
            s=dot(blk(k_vm,j),qt)
            if diag:
                kr=lax.broadcasted_iota(jnp.int32,(BLK,TQ),0); qc=lax.broadcasted_iota(jnp.int32,(BLK,TQ),1)+half*TQ
                s=jnp.where(kr<=qc,s,-1e30)
            m_new=jnp.maximum(m,jnp.max(s,axis=0,keepdims=True))
            mc=m_new*C2
            p=jnp.exp2(s*C2-mc)
            alpha=jnp.exp2(m*C2-mc)
            pb=p.astype(BF)
            p_sc[slot]=pb
            m_sc[slot]=m_new
            l=l*alpha+jnp.sum(p,axis=0,keepdims=True)
            ot_acc[...]=ot_acc[...]*alpha+dot(vt[j],pb)
            return m_new,l
        ot_acc[...]=jnp.zeros((HD,TQ),F32)
        m=jnp.full((1,TQ),-1e30,F32); l=jnp.zeros((1,TQ),F32)
        m,l=fwd(b,NB-1,True,m,l)
        m,l=lax.fori_loop(0,n_live,lambda i,c:fwd(live[i],i,False,*c),(m,l))
        inv=1.0/l
        ot=(ot_acc[...]*inv).astype(BF)
        og_ref[t,0]=ot.T.reshape(32,8,HD)
        r=jnp.sum(gt.astype(F32)*ot.astype(F32),axis=0,keepdims=True)
        mc=m*C2
        def bwd(j,slot,acc):
            f=jnp.exp2(m_sc[slot]*C2-mc)*inv
            p=p_sc[slot].astype(F32)*f
            dp=dot(blk(v_vm,j),gt)
            ds=(p*(dp-r)).astype(BF)
            rows=pl.ds(pl.multiple_of(j*BLK,BLK),BLK)
            dv_acc[rows]+=dot(p.astype(BF),g)
            dk_acc[rows]+=dot(ds,q)
            dqt_acc[...]+=dot(kt[j],ds)
        dqt_acc[...]=jnp.zeros((HD,TQ),F32)
        bwd(b,NB-1,None)
        @pl.loop(0,n_live)
        def _(i):
            bwd(live[i],i,None)
        og_ref[t,1]=(dqt_acc[...]*SCALE).astype(BF).T.reshape(32,8,HD)
        return 0
    lax.fori_loop(0,3,tile,0)
    @pl.loop(0,NB)
    def _(j):
        rows=pl.ds(pl.multiple_of(j*BLK,BLK),BLK)
        un=pl.ds(pl.multiple_of(j*64,64),64)
        k_vm[un]=(dk_acc[rows]*SCALE).astype(BF).reshape(64,8,HD)
        v_vm[un]=dv_acc[rows].astype(BF).reshape(64,8,HD)
    outs=[pltpu.make_async_copy(r.reshape(256,3,8,HD),dkv_hbm.at[:,i],sem.at[i]) for i,r in enumerate((k_vm,v_vm))]
    for l in outs: l.start()
    for l in outs: l.wait()

def attend(where,mask,kv,qg):
    return pl.pallas_call(attend_kernel,
        out_shape=(jax.ShapeDtypeStruct((256,2,3,8,HD),BF),jax.ShapeDtypeStruct((3,2,32,8,HD),BF)),
        in_specs=[pl.BlockSpec(memory_space=pltpu.SMEM)]*2+[pl.BlockSpec(memory_space=pl.ANY),pl.BlockSpec(memory_space=pltpu.VMEM)],
        out_specs=(pl.BlockSpec(memory_space=pl.ANY),pl.BlockSpec(memory_space=pltpu.VMEM)),
        scratch_shapes=[pltpu.VMEM((768,8,HD),BF)]*2+[pltpu.VMEM((NB,HD,BLK),BF)]*2+[
            pltpu.VMEM((NB,BLK,TQ),BF),pltpu.VMEM((NB,1,TQ),F32),pltpu.VMEM((NB*BLK,HD),F32),pltpu.VMEM((NB*BLK,HD),F32),
            pltpu.VMEM((HD,TQ),F32),pltpu.VMEM((HD,TQ),F32),pltpu.SMEM((16,),jnp.int32),pltpu.SemaphoreType.DMA((2,))],
        name="attend",
        compiler_params=pltpu.CompilerParams(vmem_limit_bytes=48<<20))(where,mask,kv,qg)

def place():
    ctx=lax.axis_index("ctx"); hd=lax.axis_index("head")
    return ctx//8, ctx%8, hd//8, (hd%8)//2, hd%2

def device(x, z, y, c):
    return ((x%2)*8+z, (x//2)*8+y*2+c)

def owner(tile):
    blk=tile//2; t=blk//4; bm=blk%4
    return bm+(t%2)*(3-2*bm), (tile%2+t)%2, t

def remote(src, dst, send, recv, dev):
    return pltpu.make_async_remote_copy(src_ref=src, dst_ref=dst, send_sem=send, recv_sem=recv,
                                        device_id=dev, device_id_type=pl.DeviceIdType.MESH)

def greet(x, z, y, c):
    barrier=pltpu.get_barrier_semaphore()
    def plane(i,_):
        z2=i//4; y2=i%4
        @pl.when((z2!=z)|(y2!=y))
        def _():
            pl.semaphore_signal(barrier, inc=1, device_id=device(x,z2,y2,c), device_id_type=pl.DeviceIdType.MESH)
        return 0
    lax.fori_loop(0,32,plane,0)
    def group(i,_):
        x2=i//2; c2=i%2
        @pl.when((x2!=x)|(c2!=c))
        def _():
            pl.semaphore_signal(barrier, inc=1, device_id=device(x2,z,y,c2), device_id_type=pl.DeviceIdType.MESH)
        return 0
    lax.fori_loop(0,8,group,0)

def greeted():
    pl.semaphore_wait(pltpu.get_barrier_semaphore(), 38)

ORDER=(0,1,7,2,6,3,5,4)

def gather_kernel(off, q, k, v, g, kv, qg, q_vm, k_vm, v_vm, g_vm, kv_out, qg_out, qg_in,
                  ld, a_send, a_recv, b_send, b_recv, x_send, x_recv, f_send, f_recv, c_send, c_recv, o_send, o_recv):
    x_lo,z,x_hi,y,c=place()
    x=x_hi*2+x_lo
    right=(x+1)%4; left=(x+3)%4; far=(x+2)%4
    loads=[pltpu.make_async_copy(a,b,ld.at[i]) for i,(a,b) in enumerate(((k,k_vm),(v,v_vm),(q,q_vm),(g,g_vm)))]
    for cp in loads: cp.start()
    greet(x,z,y,c)
    row=lax.broadcasted_iota(jnp.int32,(24,96),0); col=lax.broadcasted_iota(jnp.int32,(24,96),1)
    def pick(ref,h,hot):
        cols=pl.ds(pl.multiple_of(h*HD,HD),HD)
        return dot(hot,ref[:,:,cols].reshape(96,HD)).reshape(3,8,HD).astype(BF)
    def hot_of(h):
        return (col==row*4+off[h]).astype(F32).astype(BF)
    mine=z*4+y
    def to_plane(src, dst, send, recv, z2, y2, self_src):
        @pl.when((z2!=z)|(y2!=y))
        def _():
            remote(src,dst,send,recv,device(x,z2,y2,c)).start()
        @pl.when((z2==z)&(y2==y))
        def _():
            pltpu.make_async_copy(src,dst,recv).start()
    def at(ref,x2,z2,c2):
        return ref.at[x2%2,z2,x2//2,:,c2]
    loads[0].wait(); loads[1].wait()
    greeted()
    def send_kv(i,_):
        z2=(z+i//4)%8; y2=(y+i%4)%4; h=z2*4+y2
        hot=hot_of(h)
        kv_out[h,0]=pick(k_vm,h,hot)
        kv_out[h,1]=pick(v_vm,h,hot)
        to_plane(kv_out.at[h], kv.at[x_lo,z,x_hi,y,c], a_send.at[h], a_recv.at[mine], z2, y2, None)
        return 0
    lax.fori_loop(0,32,send_kv,0)
    loads[2].wait(); loads[3].wait()
    def send_qg(i,_):
        z2=(z+i//4)%8; y2=(y+i%4)%4; h=z2*4+y2
        hot=hot_of(h)
        cols=pl.ds(pl.multiple_of(h*HD,HD),HD)
        qg_out[h,0]=pick(q_vm,h,hot)
        qg_out[h,1]=g_vm[:,:,cols]
        to_plane(qg_out.at[h], qg_in.at[mine], b_send.at[h], b_recv.at[mine], z2, y2, None)
        return 0
    lax.fori_loop(0,32,send_qg,0)
    def chunk(ref,x2,z2):
        return at(ref,x2,z2,c)
    def ring(i,_):
        z2=(z+8-i)%8
        def w(j,_):
            s=z2*4+j
            pltpu.make_async_copy(kv_out.at[0],kv_out.at[0],a_recv.at[s]).wait()
            return 0
        lax.fori_loop(0,4,w,0)
        own=chunk(kv,x,z2)
        remote(own,own,x_send.at[0,z2],x_recv.at[0,z2],device(right,z,y,c)).start()
        remote(own,own,x_send.at[1,z2],x_recv.at[1,z2],device(left,z,y,c)).start()
        remote(own,own,c_send.at[x,z2],c_recv.at[x,z2],device(x,z,y,1-c)).start()
        return 0
    lax.fori_loop(0,8,ring,0)
    def halves(i,_):
        z2=(z+8-i)%8
        a=chunk(kv,left,z2); b=chunk(kv,right,z2)
        remote(a,a,x_send.at[0,z2],x_recv.at[0,z2],device(right,z,y,c)).wait_recv()
        ah=a.at[0:2]
        remote(ah,ah,f_send.at[0,z2],f_recv.at[0,z2],device(right,z,y,c)).start()
        remote(a,a,c_send.at[left,z2],c_recv.at[left,z2],device(x,z,y,1-c)).start()
        remote(b,b,x_send.at[1,z2],x_recv.at[1,z2],device(left,z,y,c)).wait_recv()
        bh=b.at[2:4]
        remote(bh,bh,f_send.at[1,z2],f_recv.at[1,z2],device(left,z,y,c)).start()
        remote(b,b,c_send.at[right,z2],c_recv.at[right,z2],device(x,z,y,1-c)).start()
        return 0
    lax.fori_loop(0,8,halves,0)
    def spread(act):
        def one(i,_):
            z2=(z+8-i//4)%8; y2=i%4; s=z2*4+y2
            act(s, ((x_lo*8+z2)*2+x_hi)*8+y2*2+c)
            return 0
        lax.fori_loop(0,32,one,0)
    def hand(s,first,count,unit,sem,op):
        tile=unit//32; u=unit%32
        xo,co,t=owner(tile)
        src=qg_in.at[s,:,pl.ds(first,count)]; dst=qg.at[t,:,pl.ds(u,count)]
        away=(xo!=x)|(co!=c)
        @pl.when(away)
        def _():
            cp=remote(src,dst,sem,o_recv.at[0],device(xo,z,y,co))
            if op=="start": cp.start()
            else: cp.wait_send()
        if op=="start":
            @pl.when((xo==x)&(co==c))
            def _():
                pltpu.make_async_copy(src,dst,o_recv.at[0]).start()
    def hand_piece(op):
        def act(s,piece):
            if op=="start":
                pltpu.make_async_copy(qg_in.at[0],qg_in.at[0],b_recv.at[s]).wait()
            unit=piece*3
            whole=(unit%32)<=29
            @pl.when(whole)
            def _():
                hand(s,0,3,unit,o_send.at[s,0],op)
            @pl.when((unit%32)>29)
            def _():
                for e in range(3):
                    hand(s,e,1,unit+e,o_send.at[s,e],op)
        return act
    spread(hand_piece("start"))
    def last(i,_):
        z2=(z+8-i)%8
        a=chunk(kv,far,z2)
        ah=a.at[0:2]; bh=a.at[2:4]
        remote(ah,ah,f_send.at[0,z2],f_recv.at[0,z2],device(right,z,y,c)).wait_recv()
        remote(bh,bh,f_send.at[1,z2],f_recv.at[1,z2],device(left,z,y,c)).wait_recv()
        remote(a,a,c_send.at[far,z2],c_recv.at[far,z2],device(x,z,y,1-c)).start()
        return 0
    lax.fori_loop(0,8,last,0)
    def sent(i,_):
        @pl.when(i!=mine)
        def _():
            pltpu.make_async_copy(kv_out.at[0],kv_out.at[0],a_send.at[i]).wait()
            pltpu.make_async_copy(qg_out.at[0],qg_out.at[0],b_send.at[i]).wait()
        return 0
    lax.fori_loop(0,32,sent,0)
    spread(hand_piece("done"))
    def ring_sent(z2,_):
        own=chunk(kv,x,z2)
        for d in range(2):
            remote(own,own,x_send.at[d,z2],x_recv.at[d,z2],device(right,z,y,c)).wait_send()
            hf=own.at[2*d:2*d+2]
            remote(hf,hf,f_send.at[d,z2],f_recv.at[d,z2],device(right,z,y,c)).wait_send()
        for x2 in range(4):
            theirs=at(kv,jnp.int32(x2),z2,1-c)
            cp=remote(theirs,theirs,c_send.at[x2,z2],c_recv.at[x2,z2],device(x,z,y,1-c))
            cp.wait_send()
            cp.wait_recv()
        return 0
    lax.fori_loop(0,8,ring_sent,0)
    pltpu.make_async_copy(qg,qg,o_recv.at[0]).wait()

KV=(2,8,2,4,2,2,3,8,HD)
DMA=pltpu.SemaphoreType.DMA
ANY=pl.BlockSpec(memory_space=pl.ANY)
def gather(off,q,k,v,g):
    return pl.pallas_call(gather_kernel,
        out_shape=(jax.ShapeDtypeStruct(KV,BF),jax.ShapeDtypeStruct((3,2,32,8,HD),BF)),
        in_specs=[pl.BlockSpec(memory_space=pltpu.SMEM)]+[ANY]*4,
        out_specs=(ANY,ANY),
        scratch_shapes=[pltpu.VMEM((24,4,4096),BF)]*3+[pltpu.VMEM((3,8,4096),BF)]+[pltpu.VMEM((32,2,3,8,HD),BF)]*3+[
            DMA((4,)),DMA((32,)),DMA((32,)),DMA((32,)),DMA((32,)),DMA((2,8)),DMA((2,8)),DMA((2,8)),DMA((2,8)),DMA((4,8)),DMA((4,8)),DMA((32,3)),DMA((1,))],
        name="gather",
        compiler_params=pltpu.CompilerParams(collective_id=0,has_side_effects=True,vmem_limit_bytes=32<<20))(off,q,k,v,g)

def scatter_kernel(dkv, og, o_out, dq_out, dk_out, dv_out,
                   own, theirs, far_in, near_in, last_in, og_in, fin,
                   ld, c_send, c_recv, g_send, g_recv, far_send, far_recv, near_send, near_recv, last_send, last_recv, p_send, p_recv):
    x_lo,z,x_hi,y,c=place()
    x=x_hi*2+x_lo
    right=(x+1)%4; left=(x+3)%4; far=(x+2)%4
    mine=z*4+y
    cols=pl.ds(pl.multiple_of(mine*HD,HD),HD)
    outs=(o_out,dq_out,dk_out,dv_out)
    def load(z2):
        return pltpu.make_async_copy(dkv.at[:,z2,:,:,c],own.at[:,z2],ld.at[z2])
    def swap(z2):
        return remote(dkv.at[:,z2,:,:,1-c],theirs.at[:,z2],c_send.at[z2],c_recv.at[z2],device(x,z,y,1-c))
    def start_load(i,_):
        load((z+i)%8).start()
        return 0
    greet(x,z,y,c)
    lax.fori_loop(0,8,start_load,0)
    greeted()
    def back(op):
        def one(i,_):
            t=i//12; e=i%12
            blk=t*4+x+(t%2)*(3-2*x)
            tile=2*blk+(c+t)%2
            def hand(unit,count,sem):
                piece=unit//3; k=unit%3; u=unit-tile*32
                xp=((piece//8)%2)*2+(piece//128)
                zp=(piece//16)%8; yp=(piece%8)//2; cp_=piece%2
                s=zp*4+yp
                src=og.at[t,:,pl.ds(u,count)]; dst=og_in.at[s,:,pl.ds(k,count)]
                away=(xp!=x)|(cp_!=c)
                @pl.when(away)
                def _():
                    cp=remote(src,dst,sem,g_recv.at[s],device(xp,z,y,cp_))
                    if op=="start": cp.start()
                    else: cp.wait_send()
                if op=="start":
                    @pl.when((xp==x)&(cp_==c))
                    def _():
                        pltpu.make_async_copy(src,dst,g_recv.at[s]).start()
            @pl.when(e<10)
            def _():
                hand(((tile*32+2)//3+e)*3,3,g_send.at[i])
            @pl.when(e>=10)
            def _():
                n=e-10; r=tile%3
                hand(tile*32+n+30*(1-(r+1)//2)+30*n*(r%2),1,g_send.at[i])
            return 0
        lax.fori_loop(0,36,one,0)
    def start_swap(i,_):
        swap((z+i)%8).start()
        return 0
    lax.fori_loop(0,8,start_swap,0)
    back("start")
    def to_rows(a, src, s):
        z2=s//4; y2=s%4
        dst=outs[a].at[:,:,cols]
        @pl.when(s!=mine)
        def _():
            remote(src,dst,p_send.at[a,s],p_recv.at[a],device(x,z2,y2,c)).start()
        @pl.when(s==mine)
        def _():
            pltpu.make_async_copy(src,dst,p_recv.at[a]).start()
    def sum_cores(i,_):
        z2=(z+i)%8
        load(z2).wait()
        swap(z2).wait_recv()
        for xl in range(2):
            for xh in range(2):
                own[xl,z2,xh]=(own[xl,z2,xh].astype(F32)+theirs[xl,z2,xh].astype(F32)).astype(BF)
        ef=own.at[far%2,z2,far//2]; er=own.at[right%2,z2,right//2]; el=own.at[left%2,z2,left//2]
        remote(ef.at[0:2],far_in.at[0,z2],far_send.at[0,z2],far_recv.at[0,z2],device(right,z,y,c)).start()
        remote(ef.at[2:4],far_in.at[1,z2],far_send.at[1,z2],far_recv.at[1,z2],device(left,z,y,c)).start()
        remote(er.at[2:4],near_in.at[0,z2],near_send.at[0,z2],near_recv.at[0,z2],device(right,z,y,c)).start()
        remote(el.at[0:2],near_in.at[1,z2],near_send.at[1,z2],near_recv.at[1,z2],device(left,z,y,c)).start()
        return 0
    lax.fori_loop(0,8,sum_cores,0)
    def rows_back(i,_):
        s=((z+i//4)%8)*4+(y+i%4)%4
        pltpu.make_async_copy(og_in.at[s],og_in.at[s],g_recv.at[s]).wait()
        to_rows(0,og_in.at[s,0],s)
        to_rows(1,og_in.at[s,1],s)
        return 0
    lax.fori_loop(0,32,rows_back,0)
    def relay(i,_):
        z2=(z+i)%8
        for d,peer in ((0,right),(1,left)):
            lo=2*d
            buf=far_in.at[d,z2]
            pltpu.make_async_copy(buf,buf,far_recv.at[d,z2]).wait()
            far_in[d,z2]=(far_in[d,z2].astype(F32)+own[peer%2,z2,peer//2,lo:lo+2].astype(F32)).astype(BF)
            remote(buf,last_in.at[d,z2],last_send.at[d,z2],last_recv.at[d,z2],device(peer,z,y,c)).start()
        return 0
    lax.fori_loop(0,8,relay,0)
    def finish(i,_):
        z2=(z+i)%8
        for d in range(2):
            pltpu.make_async_copy(last_in.at[d,z2],last_in.at[d,z2],last_recv.at[d,z2]).wait()
            pltpu.make_async_copy(near_in.at[d,z2],near_in.at[d,z2],near_recv.at[d,z2]).wait()
        for d in range(2):
            lo=2*d
            fin[z2,lo:lo+2]=(own[x_lo,z2,x_hi,lo:lo+2].astype(F32)+last_in[d,z2].astype(F32)+near_in[1-d,z2].astype(F32)).astype(BF)
        for j in range(4):
            y2=(y+j)%4
            to_rows(2,fin.at[z2,y2,0],z2*4+y2)
            to_rows(3,fin.at[z2,y2,1],z2*4+y2)
        return 0
    lax.fori_loop(0,8,finish,0)
    back("done")
    def sent(i,_):
        swap(i).wait_send()
        for d in range(2):
            b=far_in.at[d,i]
            for sem in (far_send,near_send,last_send):
                pltpu.make_async_copy(b,b,sem.at[d,i]).wait()
        return 0
    lax.fori_loop(0,8,sent,0)
    def rows_sent(i,_):
        @pl.when(i!=mine)
        def _():
            for a in range(4):
                pltpu.make_async_copy(fin.at[0,0,0],fin.at[0,0,0],p_send.at[a,i]).wait()
        return 0
    lax.fori_loop(0,32,rows_sent,0)
    for a in range(4):
        pltpu.make_async_copy(outs[a],outs[a],p_recv.at[a]).wait()

def scatter(dkv,og):
    return pl.pallas_call(scatter_kernel,
        out_shape=(jax.ShapeDtypeStruct((3,8,4096),BF),)*4,
        in_specs=[ANY]*2,
        out_specs=(ANY,)*4,
        scratch_shapes=[pltpu.VMEM((2,8,2,4,2,3,8,HD),BF)]*2+[pltpu.VMEM((2,8,2,2,3,8,HD),BF)]*3+[pltpu.VMEM((32,2,3,8,HD),BF),pltpu.VMEM((8,4,2,3,8,HD),BF),
            DMA((8,)),DMA((8,)),DMA((8,)),DMA((36,)),DMA((32,))]+[DMA((2,8))]*6+[DMA((4,32)),DMA((4,))],
        name="scatter",
        compiler_params=pltpu.CompilerParams(collective_id=1,has_side_effects=True,vmem_limit_bytes=32<<20))(dkv,og)

def on_device(queries,key_states,value_states,out_grad,offsets,block_mask):
    kv,qg=gather(offsets,queries,key_states,value_states,out_grad.reshape(3,8,4096))
    x_lo,z,x_hi,y,c=place()
    where=jnp.stack([x_hi*2+x_lo,c]).astype(jnp.int32)
    dkv,og=attend(where,block_mask,kv.reshape(256,2,3,8,HD),qg)
    outs=scatter(dkv.reshape(KV),og)
    return tuple(o.reshape(24,4096) for o in outs)


def solution(mesh):
    rows3=P(("ctx","head"),None,None); rows2=P(("ctx","head"),None)
    return jax.shard_map(on_device,mesh=mesh,in_specs=(rows3,rows3,rows3,rows2,P(),P()),
                         out_specs=(rows2,)*4,check_vma=False)
```

```python
import functools, jax, jax.numpy as jnp
from jax.sharding import PartitionSpec as P
from jax import lax
from jax.experimental import pallas as pl
from jax.experimental.pallas import tpu as pltpu
BF=jnp.bfloat16; F32=jnp.float32
HEADS=32; NB=12; BLK=512; TQ=256; HD=128
SCALE=HD**-0.5
C2=SCALE*1.4426950408889634
GF=2; GB=2

def dot(a,b):
    return jnp.dot(a,b,preferred_element_type=F32)

def dot_t(a,b):
    return lax.dot_general(a,b,(((0,),(0,)),((),())),preferred_element_type=F32)

def my_tiles():
    ctx=lax.axis_index("ctx"); hd=lax.axis_index("head")
    return (hd//8)*2+ctx//8, hd%2

def attend_kernel(mask_hbm, kv_ref, qg_ref, dkv_ref, og_ref,
                  p_sc, m_sc, dk_acc, dv_acc, ot_acc, dqt_acc, live, mask_ref, ld):
    grp,core=my_tiles()
    fetch=pltpu.make_async_copy(mask_hbm,mask_ref,ld.at[0])
    fetch.start()
    kv_rows=kv_ref.reshape(2,768,8,HD)
    dkv_rows=dkv_ref.reshape(2,768,8,HD)
    def blk(i,j):
        return kv_rows[i,pl.ds(pl.multiple_of(j*64,64),64)].reshape(BLK,HD)
    @pl.loop(0,NB)
    def _(j):
        z=jnp.zeros((BLK,HD),F32)
        rows=pl.ds(pl.multiple_of(j*BLK,BLK),BLK)
        dk_acc[rows]=z; dv_acc[rows]=z
    def tile(t):
        bm=grp
        b=t*4+bm+(t%2)*(3-2*bm)
        half=(core+t)%2
        q=qg_ref[t,0].reshape(TQ,HD); g=qg_ref[t,1].reshape(TQ,HD)
        qt=q.T; gt=g.T
        def count(j,n):
            live[n]=j
            return n+mask_ref[b,j]
        n_live=lax.fori_loop(0,b,count,0)
        def fwd(js,slots,diag,m,l):
            ss=[]
            for j in js:
                s=dot(blk(0,j),qt)
                if diag:
                    kr=lax.broadcasted_iota(jnp.int32,(BLK,TQ),0); qc=lax.broadcasted_iota(jnp.int32,(BLK,TQ),1)+half*TQ
                    s=jnp.where(kr<=qc,s,-1e30)
                ss.append(s)
            m_new=m
            for s in ss: m_new=jnp.maximum(m_new,jnp.max(s,axis=0,keepdims=True))
            mc=m_new*C2
            alpha=jnp.exp2(m*C2-mc)
            l=l*alpha
            acc=ot_acc[...]*alpha
            for j,slot,s in zip(js,slots,ss):
                p=jnp.exp2(s*C2-mc)
                pb=p.astype(BF)
                p_sc[slot]=pb
                m_sc[slot]=m_new
                l=l+jnp.sum(p,axis=0,keepdims=True)
                acc=acc+dot_t(blk(1,j),pb)
            ot_acc[...]=acc
            return m_new,l
        def run(group,step,carry):
            whole=n_live//group
            def body(i,c):
                idx=[i*group+e for e in range(group)]
                return step([live[e] for e in idx],idx,c)
            carry=lax.fori_loop(0,whole,body,carry)
            if group>1:
                carry=lax.fori_loop(whole*group,n_live,lambda i,c: step([live[i]],[i],c),carry)
            return carry
        ot_acc[...]=jnp.zeros((HD,TQ),F32)
        m=jnp.full((1,TQ),-1e30,F32); l=jnp.zeros((1,TQ),F32)
        m,l=fwd([b],[NB-1],True,m,l)
        m,l=run(GF,lambda js,sl,c: fwd(js,sl,False,*c),(m,l))
        inv=1.0/l
        ot=(ot_acc[...]*inv).astype(BF)
        og_ref[t,0]=ot.T.reshape(32,8,HD)
        r=jnp.sum(gt.astype(F32)*ot.astype(F32),axis=0,keepdims=True)
        mc=m*C2
        def bwd(js,slots,c):
            acc=dqt_acc[...]
            for j,slot in zip(js,slots):
                f=jnp.exp2(m_sc[slot]*C2-mc)*inv
                p=p_sc[slot].astype(F32)*f
                dp=dot(blk(1,j),gt)
                ds=(p*(dp-r)).astype(BF)
                rows=pl.ds(pl.multiple_of(j*BLK,BLK),BLK)
                dv_acc[rows]+=dot(p.astype(BF),g)
                dk_acc[rows]+=dot(ds,q)
                acc=acc+dot_t(blk(0,j),ds)
            dqt_acc[...]=acc
            return c
        dqt_acc[...]=jnp.zeros((HD,TQ),F32)
        bwd([b],[NB-1],0)
        run(GB,bwd,0)
        og_ref[t,1]=(dqt_acc[...]*SCALE).astype(BF).T.reshape(32,8,HD)
    def settle_blocks(lo,hi):
        @pl.loop(lo,hi)
        def _(j):
            rows=pl.ds(pl.multiple_of(j*BLK,BLK),BLK)
            un=pl.ds(pl.multiple_of(j*64,64),64)
            dkv_rows[0,un]=(dk_acc[rows]*SCALE).astype(BF).reshape(64,8,HD)
            dkv_rows[1,un]=dv_acc[rows].astype(BF).reshape(64,8,HD)
    fetch.wait()
    @pl.loop(0,3)
    def _(t):
        tile(t)
    settle_blocks(0,NB)

KV=(2,2,8,2,4,2,3,8,HD)
QG=(3,2,32,8,HD)
VM=pl.BlockSpec(memory_space=pltpu.VMEM)
ANY=pl.BlockSpec(memory_space=pl.ANY)
DMA=pltpu.SemaphoreType.DMA
def held(x):
    return pltpu.with_memory_space_constraint(x,pltpu.VMEM)
def afar(x):
    return pltpu.with_memory_space_constraint(x,pltpu.HBM)
def attend(mask,kv,qg):
    return pl.pallas_call(attend_kernel,
        out_shape=(pltpu.VMEM(KV,BF),pltpu.VMEM(QG,BF)),
        in_specs=[ANY,VM,VM],
        out_specs=(VM,VM),
        scratch_shapes=[
            pltpu.VMEM((NB,BLK,TQ),BF),pltpu.VMEM((NB,1,TQ),F32),pltpu.VMEM((NB*BLK,HD),F32),pltpu.VMEM((NB*BLK,HD),F32),
            pltpu.VMEM((HD,TQ),F32),pltpu.VMEM((HD,TQ),F32),pltpu.SMEM((16,),jnp.int32),pltpu.SMEM((NB,NB),jnp.int32),DMA((1,))],
        name="attend",
        compiler_params=pltpu.CompilerParams(vmem_limit_bytes=40<<20))(afar(mask),held(kv),held(qg))

MESH=pl.DeviceIdType.MESH

def place():
    ctx=lax.axis_index("ctx"); hd=lax.axis_index("head")
    return ctx//8, ctx%8, hd//8, (hd%8)//2, hd%2

def device(x, z, y, c):
    return ((x%2)*8+z, (x//2)*8+y*2+c)

def owner(tile):
    blk=tile//2; t=blk//4; bm=blk%4
    return bm+(t%2)*(3-2*bm), (tile%2+t)%2, t

def order(i):
    return (i%2)*((i+1)//2)+(1-i%2)*((8-i//2)%8)

def remote(src, dst, send, recv, dev):
    return pltpu.make_async_remote_copy(src_ref=src, dst_ref=dst, send_sem=send, recv_sem=recv,
                                        device_id=dev, device_id_type=MESH)

def wait_for(ref, sem):
    pltpu.make_async_copy(ref,ref,sem).wait()

def greet(x, z, y, c):
    barrier=pltpu.get_barrier_semaphore()
    def plane(i,_):
        s=(z*4+y+i)%32
        pl.semaphore_signal(barrier, inc=1, device_id=device(x,s//4,s%4,c), device_id_type=MESH)
        return 0
    lax.fori_loop(1,32,plane,0,unroll=True)
    for i in range(1,8):
        s=(x*2+c+i)%8
        pl.semaphore_signal(barrier, inc=1, device_id=device(s//2,z,y,s%2), device_id_type=MESH)

def greeted():
    pl.semaphore_wait(pltpu.get_barrier_semaphore(), 38)

def gather_kernel(off_hbm, q, k, v, g, kv, qg, q_vm, k_vm, v_vm, g_vm, kv_out, qg_out, qg_in,
                  off, ld, a_send, a_recv, b_send, b_recv, x_send, x_recv, f_send, f_recv, c_send, c_recv, o_send, o_recv):
    x_lo,z,x_hi,y,c=place()
    x=x_hi*2+x_lo
    right=(x+1)%4; left=(x+3)%4; far=(x+2)%4
    mine=z*4+y
    for i in range(8):
        cols=pl.ds(pl.multiple_of(((z+order(i))%8)*512,512),512)
        pltpu.make_async_copy(k.at[:,:,cols],k_vm.at[:,:,cols],ld.at[i]).start()
        pltpu.make_async_copy(v.at[:,:,cols],v_vm.at[:,:,cols],ld.at[i]).start()
    pltpu.make_async_copy(q,q_vm,ld.at[8]).start()
    pltpu.make_async_copy(g,g_vm,ld.at[9]).start()
    fetch=pltpu.make_async_copy(off_hbm,off,ld.at[10])
    fetch.start()
    greet(x,z,y,c)
    row=lax.broadcasted_iota(jnp.int32,(24,96),0); col=lax.broadcasted_iota(jnp.int32,(24,96),1)
    lead=col-row*4
    def columns(h):
        return pl.ds(pl.multiple_of(h*HD,HD),HD)
    def pick(ref,h,hot):
        return dot(hot,ref[:,:,columns(h)].reshape(96,HD)).reshape(3,8,HD).astype(BF)
    def hot_of(h):
        return (lead==off[h]).astype(F32).astype(BF)
    def chunk(x2,z2):
        return kv.at[:,x2%2,z2,x2//2,:,c]
    def pick_kv(i):
        wait_for(k_vm.at[:,:,pl.ds(0,1024)],ld.at[i])
        z2=(z+order(i))%8
        for j in range(4):
            h=z2*4+(y+j)%4
            hot=hot_of(h)
            kv_out[h,0]=pick(k_vm,h,hot)
            kv_out[h,1]=pick(v_vm,h,hot)
    def pick_qg(i):
        z2=(z+order(i))%8
        for j in range(4):
            h=z2*4+(y+j)%4
            qg_out[h,0]=pick(q_vm,h,hot_of(h))
            qg_out[h,1]=g_vm[:,:,columns(h)]
    def to_plane(i, out, dst, send, recv):
        z2=(z+order(i))%8
        for j in range(4):
            y2=(y+j)%4
            src=out.at[z2*4+y2]
            if isinstance(i,int) and i==0 and j==0:
                pltpu.make_async_copy(src,dst,recv).start()
            else:
                remote(src,dst,send,recv,device(x,z2,y2,c)).start()
    def send_kv(i):
        to_plane(i,kv_out,kv.at[:,x_lo,z,x_hi,y,c],a_send.at[0],a_recv.at[i])
    def send_qg(i):
        to_plane(i,qg_out,qg_in.at[mine],b_send.at[0],b_recv.at[i])
    def ring(i):
        z2=(z+8-order(i))%8
        wait_for(kv_out.at[0:4],a_recv.at[i])
        own=chunk(x,z2)
        remote(own,own,x_send.at[0],x_recv.at[0,i],device(right,z,y,c)).start()
        remote(own,own,x_send.at[1],x_recv.at[1,i],device(left,z,y,c)).start()
        remote(own,own,c_send.at[0],c_recv.at[0],device(x,z,y,1-c)).start()
    def halves(i):
        z2=(z+8-order(i))%8
        for d,frm,to in ((0,left,right),(1,right,left)):
            a=chunk(frm,z2)
            wait_for(a,x_recv.at[d,i])
            ah=a.at[:,2*d:2*d+2]
            remote(ah,ah,f_send.at[d],f_recv.at[i],device(to,z,y,c)).start()
            remote(a,a,c_send.at[0],c_recv.at[0],device(x,z,y,1-c)).start()
    def last(i):
        z2=(z+8-order(i))%8
        a=chunk(far,z2)
        wait_for(a,f_recv.at[i])
        remote(a,a,c_send.at[0],c_recv.at[0],device(x,z,y,1-c)).start()
    def hand(s,first,count,unit,op):
        tile=unit//32; u=unit%32
        xo,co,t=owner(tile)
        src=qg_in.at[s,:,pl.ds(first,count)]; dst=qg.at[t,:,pl.ds(u,count)]
        @pl.when((xo!=x)|(co!=c))
        def _():
            cp=remote(src,dst,o_send.at[0],o_recv.at[0],device(xo,z,y,co))
            if op=="start": cp.start()
            else: cp.wait_send()
        if op=="start":
            @pl.when((xo==x)&(co==c))
            def _():
                pltpu.make_async_copy(src,dst,o_recv.at[0]).start()
    def spread(i,op):
        z2=(z+8-order(i))%8
        if op=="start":
            wait_for(qg_in.at[0:4],b_recv.at[i])
        def one(y2,_):
            s=z2*4+y2
            unit=(((x_lo*8+z2)*2+x_hi)*8+y2*2+c)*3
            @pl.when((unit%32)<=29)
            def _():
                hand(s,0,3,unit,op)
            @pl.when((unit%32)>29)
            def _():
                for e in range(3):
                    hand(s,e,1,unit+e,op)
            return 0
        lax.fori_loop(0,4,one,0)
    def loop(lo,hi,*acts):
        def body(i,_):
            for act in acts: act(i)
            return 0
        lax.fori_loop(lo,hi,body,0)
    def seq(lo,hi,*acts):
        loop(lo,hi,*[(lambda i,f=f,d=d: f(i+d)) for f,d in acts])
    def spread_start(i):
        spread(i,"start")
    fetch.wait()
    pick_kv(0)
    greeted()
    send_kv(0)
    loop(1,8,pick_kv,send_kv)
    wait_for(q_vm,ld.at[8]); wait_for(g_vm,ld.at[9])
    pick_qg(0); send_qg(0); ring(0)
    loop(1,8,pick_qg,send_qg,ring)
    loop(0,4,halves)
    seq(4,8,(halves,0),(spread_start,-4))
    seq(0,4,(last,0),(spread_start,4))
    loop(4,8,last)
    wait_for(kv_out.at[0:31],a_send.at[0])
    wait_for(qg_out.at[0:31],b_send.at[0])
    loop(0,8,lambda i: spread(i,"done"))
    for d in range(2):
        wait_for(kv.at[:,0,:,0,:,0],x_send.at[d])
        wait_for(kv.at[:,0,:,0,0:2,0],f_send.at[d])
    wait_for(kv.at[:,:,:,:,:,0],c_send.at[0])
    wait_for(kv.at[:,:,:,:,:,0],c_recv.at[0])
    wait_for(qg,o_recv.at[0])

def gather(off,q,k,v,g):
    return pl.pallas_call(gather_kernel,
        out_shape=(pltpu.VMEM(KV,BF),pltpu.VMEM(QG,BF)),
        in_specs=[ANY]*5,
        out_specs=(VM,VM),
        scratch_shapes=[pltpu.VMEM((24,4,4096),BF)]*3+[pltpu.VMEM((3,8,4096),BF)]+[pltpu.VMEM((32,2,3,8,HD),BF)]*3+[
            pltpu.SMEM((HEADS,),jnp.int32),DMA((11,)),DMA((1,)),DMA((8,)),DMA((1,)),DMA((8,)),DMA((2,)),DMA((2,8)),DMA((2,)),DMA((8,)),DMA((1,)),DMA((1,)),DMA((1,)),DMA((1,))],
        name="gather",
        compiler_params=pltpu.CompilerParams(collective_id=0,has_side_effects=True,vmem_limit_bytes=40<<20))(*[afar(a) for a in (off,q,k,v,g)])

def scatter_kernel(dkv, og, o_out, dq_out, dk_out, dv_out,
                   own, far_in, near_in, last_in, og_in, fin,
                   c_send, c_recv, g_send, g_recv, far_send, far_recv, near_send, last_send, fin_recv, p_send, p_recv):
    x_lo,z,x_hi,y,c=place()
    x=x_hi*2+x_lo
    right=(x+1)%4; left=(x+3)%4; far=(x+2)%4
    mine=z*4+y
    cols=pl.ds(pl.multiple_of(mine*HD,HD),HD)
    outs=(o_out,dq_out,dk_out,dv_out)
    def at_z(i):
        return (z+order(i))%8
    greet(x,z,y,c)
    greeted()
    def back(op):
        def one(i,_):
            t=i//12; e=i%12
            blk=t*4+x+(t%2)*(3-2*x)
            tile=2*blk+(c+t)%2
            def hand(unit,count):
                piece=unit//3; k=unit%3; u=unit-tile*32
                xp=((piece//8)%2)*2+(piece//128)
                zp=(piece//16)%8; yp=(piece%8)//2; cp_=piece%2
                s=zp*4+yp
                src=og.at[t,:,pl.ds(u,count)]; dst=og_in.at[s,:,pl.ds(k,count)]
                sem=g_recv.at[zp]
                @pl.when((xp!=x)|(cp_!=c))
                def _():
                    cp=remote(src,dst,g_send.at[0],sem,device(xp,z,y,cp_))
                    if op=="start": cp.start()
                    else: cp.wait_send()
                if op=="start":
                    @pl.when((xp==x)&(cp_==c))
                    def _():
                        pltpu.make_async_copy(src,dst,sem).start()
            @pl.when(e<10)
            def _():
                hand(((tile*32+2)//3+e)*3,3)
            @pl.when(e>=10)
            def _():
                n=e-10; r=tile%3
                hand(tile*32+n+30*(1-(r+1)//2)+30*n*(r%2),1)
            return 0
        lax.fori_loop(0,36,one,0)
    for i in range(8):
        z2=at_z(i)
        remote(dkv.at[:,:,z2,:,:,1-c],own.at[:,:,z2],c_send.at[0],c_recv.at[i],device(x,z,y,1-c)).start()
    back("start")
    def to_rows(a, src, sem, s, i, j):
        dst=outs[a].at[:,:,cols]
        if isinstance(i,int) and i==0 and j==0:
            pltpu.make_async_copy(src,dst,p_recv.at[a]).start()
        else:
            remote(src,dst,sem,p_recv.at[a],device(x,s//4,s%4,c)).start()
    def sum_cores(i):
        z2=at_z(i)
        wait_for(own.at[:,:,z2],c_recv.at[i])
        for xl in range(2):
            for xh in range(2):
                own[:,xl,z2,xh]=(own[:,xl,z2,xh].astype(F32)+dkv[:,xl,z2,xh,:,c].astype(F32)).astype(BF)
        ef=own.at[:,far%2,z2,far//2]; er=own.at[:,right%2,z2,right//2]; el=own.at[:,left%2,z2,left//2]
        remote(ef.at[:,0:2],far_in.at[0,z2],far_send.at[0],far_recv.at[0,i],device(right,z,y,c)).start()
        remote(ef.at[:,2:4],far_in.at[1,z2],far_send.at[0],far_recv.at[1,i],device(left,z,y,c)).start()
        remote(er.at[:,2:4],near_in.at[0,z2],near_send.at[0],fin_recv.at[i],device(right,z,y,c)).start()
        remote(el.at[:,0:2],near_in.at[1,z2],near_send.at[0],fin_recv.at[i],device(left,z,y,c)).start()
    def rows_back(i):
        z2=at_z(i)
        wait_for(og_in.at[0:4],g_recv.at[z2])
        for j in range(4):
            s=z2*4+(y+j)%4
            to_rows(0,og_in.at[s,0],p_send.at[0],s,i,j)
            to_rows(1,og_in.at[s,1],p_send.at[0],s,i,j)
    def relay(i):
        z2=at_z(i)
        for d,peer in ((0,right),(1,left)):
            lo=2*d
            buf=far_in.at[d,z2]
            wait_for(buf,far_recv.at[d,i])
            far_in[d,z2]=(far_in[d,z2].astype(F32)+own[:,peer%2,z2,peer//2,lo:lo+2].astype(F32)).astype(BF)
            remote(buf,last_in.at[d,z2],last_send.at[0],fin_recv.at[i],device(peer,z,y,c)).start()
    def finish(i):
        z2=at_z(i)
        wait_for(own.at[:,0,z2],fin_recv.at[i])
        for d in range(2):
            lo=2*d
            fin[:,pl.ds(z2*4+lo,2)]=(own[:,x_lo,z2,x_hi,lo:lo+2].astype(F32)+last_in[d,z2].astype(F32)+near_in[1-d,z2].astype(F32)).astype(BF)
        for j in range(4):
            s=z2*4+(y+j)%4
            to_rows(2,fin.at[0,s],p_send.at[1],s,i,j)
            to_rows(3,fin.at[1,s],p_send.at[1],s,i,j)
    def loop(lo,hi,*acts):
        def body(i,_):
            for act in acts: act(i)
            return 0
        lax.fori_loop(lo,hi,body,0)
    sum_cores(0)
    rows_back(0)
    loop(1,8,sum_cores,rows_back)
    loop(0,2,relay)
    relay(2); finish(0)
    loop(3,8,relay,lambda i: finish(i-2))
    loop(6,8,finish)
    back("done")
    wait_for(own,c_send.at[0])
    for b,sem in ((far_in,far_send),(near_in,near_send),(last_in,last_send)):
        wait_for(b,sem.at[0])
    wait_for(og_in.at[0:31],p_send.at[0])
    wait_for(fin.at[:,0:31],p_send.at[1])
    for a in range(4):
        wait_for(outs[a],p_recv.at[a])

def scatter(dkv,og):
    return pl.pallas_call(scatter_kernel,
        out_shape=(pltpu.VMEM((3,8,4096),BF),)*4,
        in_specs=[VM]*2,
        out_specs=(VM,)*4,
        scratch_shapes=[pltpu.VMEM((2,2,8,2,4,3,8,HD),BF)]+[pltpu.VMEM((2,8,2,2,3,8,HD),BF)]*3+[pltpu.VMEM((32,2,3,8,HD),BF),pltpu.VMEM((2,32,3,8,HD),BF),
            DMA((1,)),DMA((8,)),DMA((1,)),DMA((8,)),DMA((1,)),DMA((2,8)),DMA((1,)),DMA((1,)),DMA((8,)),DMA((2,)),DMA((4,))],
        name="scatter",
        compiler_params=pltpu.CompilerParams(collective_id=1,has_side_effects=True,vmem_limit_bytes=40<<20))(held(dkv),held(og))

def settle_kernel(*refs):
    sem=refs[8]
    cps=[pltpu.make_async_copy(refs[i],refs[4+i],sem.at[i]) for i in range(4)]
    for cp in cps: cp.start()
    for cp in cps: cp.wait()

def settle(outs):
    return pl.pallas_call(settle_kernel,
        out_shape=(jax.ShapeDtypeStruct((3,8,4096),BF),)*4,
        in_specs=[VM]*4,out_specs=(ANY,)*4,
        scratch_shapes=[DMA((4,))],
        name="settle",
        compiler_params=pltpu.CompilerParams(vmem_limit_bytes=40<<20))(*[held(o) for o in outs])

def on_device(queries,key_states,value_states,out_grad,offsets,block_mask):
    kv,qg=gather(offsets,queries,key_states,value_states,out_grad.reshape(3,8,4096))
    dkv,og=attend(block_mask,kv,qg)
    outs=settle(scatter(dkv,og))
    return tuple(o.reshape(24,4096) for o in outs)


def solution(mesh):
    rows3=P(("ctx","head"),None,None); rows2=P(("ctx","head"),None)
    return jax.shard_map(on_device,mesh=mesh,in_specs=(rows3,rows3,rows3,rows2,P(),P()),
                         out_specs=(rows2,)*4,check_vma=False)
```

```python
import functools, jax, jax.numpy as jnp
from jax.sharding import PartitionSpec as P
from jax import lax
from jax.experimental import pallas as pl
from jax.experimental.pallas import tpu as pltpu
BF=jnp.bfloat16; F32=jnp.float32
HEADS=32; NB=12; BLK=512; TQ=256; HD=128
SCALE=HD**-0.5
C2=SCALE*1.4426950408889634
GF=2; GB=2

def dot(a,b):
    return jnp.dot(a,b,preferred_element_type=F32)

def dot_t(a,b):
    return lax.dot_general(a,b,(((0,),(0,)),((),())),preferred_element_type=F32)

def my_tiles():
    ctx=lax.axis_index("ctx"); hd=lax.axis_index("head")
    return (hd//8)*2+ctx//8, hd%2

def attend_kernel(mask_hbm, kv_ref, qg_ref, dkv_ref, og_ref,
                  p_sc, m_sc, dk_acc, dv_acc, ot_acc, dqt_acc, live, mask_ref, ld):
    grp,core=my_tiles()
    fetch=pltpu.make_async_copy(mask_hbm,mask_ref,ld.at[0])
    fetch.start()
    kv_rows=kv_ref.reshape(2,768,8,HD)
    dkv_rows=dkv_ref.reshape(2,768,8,HD)
    def blk(i,j):
        return kv_rows[i,pl.ds(pl.multiple_of(j*64,64),64)].reshape(BLK,HD)
    @pl.loop(0,NB)
    def _(j):
        z=jnp.zeros((BLK,HD),F32)
        rows=pl.ds(pl.multiple_of(j*BLK,BLK),BLK)
        dk_acc[rows]=z; dv_acc[rows]=z
    def tile(t):
        bm=grp
        b=t*4+bm+(t%2)*(3-2*bm)
        half=(core+t)%2
        q=qg_ref[t,0].reshape(TQ,HD); g=qg_ref[t,1].reshape(TQ,HD)
        qt=q.T; gt=g.T
        def count(j,n):
            live[n]=j
            return n+mask_ref[b,j]
        n_live=lax.fori_loop(0,b,count,0)
        def fwd(js,slots,diag,m,l):
            ss=[]
            for j in js:
                s=dot(blk(0,j),qt)
                if diag:
                    kr=lax.broadcasted_iota(jnp.int32,(BLK,TQ),0); qc=lax.broadcasted_iota(jnp.int32,(BLK,TQ),1)+half*TQ
                    s=jnp.where(kr<=qc,s,-1e30)
                ss.append(s)
            m_new=m
            for s in ss: m_new=jnp.maximum(m_new,jnp.max(s,axis=0,keepdims=True))
            mc=m_new*C2
            alpha=jnp.exp2(m*C2-mc)
            l=l*alpha
            acc=ot_acc[...]*alpha
            for j,slot,s in zip(js,slots,ss):
                p=jnp.exp2(s*C2-mc)
                pb=p.astype(BF)
                p_sc[slot]=pb
                m_sc[slot]=m_new
                l=l+jnp.sum(p,axis=0,keepdims=True)
                acc=acc+dot_t(blk(1,j),pb)
            ot_acc[...]=acc
            return m_new,l
        def run(group,step,carry):
            whole=n_live//group
            def body(i,c):
                idx=[i*group+e for e in range(group)]
                return step([live[e] for e in idx],idx,c)
            carry=lax.fori_loop(0,whole,body,carry)
            if group>1:
                carry=lax.fori_loop(whole*group,n_live,lambda i,c: step([live[i]],[i],c),carry)
            return carry
        ot_acc[...]=jnp.zeros((HD,TQ),F32)
        m=jnp.full((1,TQ),-1e30,F32); l=jnp.zeros((1,TQ),F32)
        m,l=fwd([b],[NB-1],True,m,l)
        m,l=run(GF,lambda js,sl,c: fwd(js,sl,False,*c),(m,l))
        inv=1.0/l
        ot=(ot_acc[...]*inv).astype(BF)
        og_ref[t,0]=ot.T.reshape(32,8,HD)
        r=jnp.sum(gt.astype(F32)*ot.astype(F32),axis=0,keepdims=True)
        mc=m*C2
        def bwd(js,slots,c):
            acc=dqt_acc[...]
            for j,slot in zip(js,slots):
                f=jnp.exp2(m_sc[slot]*C2-mc)*inv
                p=p_sc[slot].astype(F32)*f
                dp=dot(blk(1,j),gt)
                ds=(p*(dp-r)).astype(BF)
                rows=pl.ds(pl.multiple_of(j*BLK,BLK),BLK)
                dv_acc[rows]+=dot(p.astype(BF),g)
                dk_acc[rows]+=dot(ds,q)
                acc=acc+dot_t(blk(0,j),ds)
            dqt_acc[...]=acc
            return c
        dqt_acc[...]=jnp.zeros((HD,TQ),F32)
        bwd([b],[NB-1],0)
        run(GB,bwd,0)
        og_ref[t,1]=(dqt_acc[...]*SCALE).astype(BF).T.reshape(32,8,HD)
    def settle_blocks(lo,hi):
        @pl.loop(lo,hi)
        def _(j):
            rows=pl.ds(pl.multiple_of(j*BLK,BLK),BLK)
            un=pl.ds(pl.multiple_of(j*64,64),64)
            dkv_rows[0,un]=(dk_acc[rows]*SCALE).astype(BF).reshape(64,8,HD)
            dkv_rows[1,un]=dv_acc[rows].astype(BF).reshape(64,8,HD)
    fetch.wait()
    @pl.loop(0,3)
    def _(t):
        tile(t)
    settle_blocks(0,NB)

KV=(2,2,8,2,4,2,3,8,HD)
QG=(3,2,32,8,HD)
VM=pl.BlockSpec(memory_space=pltpu.VMEM)
ANY=pl.BlockSpec(memory_space=pl.ANY)
DMA=pltpu.SemaphoreType.DMA
def held(x):
    return pltpu.with_memory_space_constraint(x,pltpu.VMEM)
def afar(x):
    return pltpu.with_memory_space_constraint(x,pltpu.HBM)
def attend(mask,kv,qg):
    return pl.pallas_call(attend_kernel,
        out_shape=(pltpu.VMEM(KV,BF),pltpu.VMEM(QG,BF)),
        in_specs=[ANY,VM,VM],
        out_specs=(VM,VM),
        scratch_shapes=[
            pltpu.VMEM((NB,BLK,TQ),BF),pltpu.VMEM((NB,1,TQ),F32),pltpu.VMEM((NB*BLK,HD),F32),pltpu.VMEM((NB*BLK,HD),F32),
            pltpu.VMEM((HD,TQ),F32),pltpu.VMEM((HD,TQ),F32),pltpu.SMEM((16,),jnp.int32),pltpu.SMEM((NB,NB),jnp.int32),DMA((1,))],
        name="attend",
        compiler_params=pltpu.CompilerParams(vmem_limit_bytes=40<<20))(afar(mask),held(kv),held(qg))

MESH=pl.DeviceIdType.MESH

def place():
    ctx=lax.axis_index("ctx"); hd=lax.axis_index("head")
    return ctx//8, ctx%8, hd//8, (hd%8)//2, hd%2

def device(x, z, y, c):
    return ((x%2)*8+z, (x//2)*8+y*2+c)

def owner(tile):
    blk=tile//2; t=blk//4; bm=blk%4
    return bm+(t%2)*(3-2*bm), (tile%2+t)%2, t

def order(i):
    return (i%2)*((i+1)//2)+(1-i%2)*((8-i//2)%8)

def remote(src, dst, send, recv, dev):
    return pltpu.make_async_remote_copy(src_ref=src, dst_ref=dst, send_sem=send, recv_sem=recv,
                                        device_id=dev, device_id_type=MESH)

def wait_for(ref, sem):
    pltpu.make_async_copy(ref,ref,sem).wait()

def greet(x, z, y, c):
    barrier=pltpu.get_barrier_semaphore()
    def plane(i,_):
        s=(z*4+y+i)%32
        pl.semaphore_signal(barrier, inc=1, device_id=device(x,s//4,s%4,c), device_id_type=MESH)
        return 0
    lax.fori_loop(1,32,plane,0,unroll=True)
    for i in range(1,8):
        s=(x*2+c+i)%8
        pl.semaphore_signal(barrier, inc=1, device_id=device(s//2,z,y,s%2), device_id_type=MESH)

def greeted():
    pl.semaphore_wait(pltpu.get_barrier_semaphore(), 38)

def gather_kernel(off_hbm, q, k, v, g, kv, qg, q_vm, k_vm, v_vm, g_vm, kv_out, qg_out, qg_in,
                  off, ld, a_send, a_recv, b_send, b_recv, x_send, x_recv, f_send, f_recv, c_send, c_recv, o_send, o_recv):
    x_lo,z,x_hi,y,c=place()
    x=x_hi*2+x_lo
    right=(x+1)%4; left=(x+3)%4; far=(x+2)%4
    mine=z*4+y
    for i in range(8):
        cols=pl.ds(pl.multiple_of(((z+order(i))%8)*512,512),512)
        pltpu.make_async_copy(k.at[:,:,cols],k_vm.at[:,:,cols],ld.at[i]).start()
        pltpu.make_async_copy(v.at[:,:,cols],v_vm.at[:,:,cols],ld.at[i]).start()
    pltpu.make_async_copy(q,q_vm,ld.at[8]).start()
    pltpu.make_async_copy(g,g_vm,ld.at[9]).start()
    fetch=pltpu.make_async_copy(off_hbm,off,ld.at[10])
    fetch.start()
    greet(x,z,y,c)
    row=lax.broadcasted_iota(jnp.int32,(24,96),0); col=lax.broadcasted_iota(jnp.int32,(24,96),1)
    lead=col-row*4
    def columns(h):
        return pl.ds(pl.multiple_of(h*HD,HD),HD)
    def pick(ref,h,hot):
        return dot(hot,ref[:,:,columns(h)].reshape(96,HD)).reshape(3,8,HD).astype(BF)
    def hot_of(h):
        return (lead==off[h]).astype(F32).astype(BF)
    def chunk(x2,z2):
        return kv.at[:,x2%2,z2,x2//2,:,c]
    def pick_kv(i):
        wait_for(k_vm.at[:,:,pl.ds(0,1024)],ld.at[i])
        z2=(z+order(i))%8
        for j in range(4):
            h=z2*4+(y+j)%4
            hot=hot_of(h)
            kv_out[h,0]=pick(k_vm,h,hot)
            kv_out[h,1]=pick(v_vm,h,hot)
    def pick_qg(i):
        z2=(z+order(i))%8
        for j in range(4):
            h=z2*4+(y+j)%4
            qg_out[h,0]=pick(q_vm,h,hot_of(h))
            qg_out[h,1]=g_vm[:,:,columns(h)]
    def to_plane(i, out, dst, send, recv):
        z2=(z+order(i))%8
        for j in range(4):
            y2=(y+j)%4
            src=out.at[z2*4+y2]
            if j:
                remote(src,dst,send,recv,device(x,z2,y2,c)).start()
            else:
                @pl.when(z2!=z)
                def _():
                    remote(src,dst,send,recv,device(x,z2,y2,c)).start()
                @pl.when(z2==z)
                def _():
                    pltpu.make_async_copy(src,dst,recv).start()
    def send_kv(i):
        to_plane(i,kv_out,kv.at[:,x_lo,z,x_hi,y,c],a_send.at[0],a_recv.at[i])
    def send_qg(i):
        to_plane(i,qg_out,qg_in.at[mine],b_send.at[0],b_recv.at[i])
    def ring(i):
        z2=(z+8-order(i))%8
        wait_for(kv_out.at[0:4],a_recv.at[i])
        own=chunk(x,z2)
        remote(own,own,x_send.at[0],x_recv.at[0,i],device(right,z,y,c)).start()
        remote(own,own,x_send.at[1],x_recv.at[1,i],device(left,z,y,c)).start()
        remote(own,own,c_send.at[0],c_recv.at[0],device(x,z,y,1-c)).start()
    def halves(i):
        z2=(z+8-order(i))%8
        for d,frm,to in ((0,left,right),(1,right,left)):
            a=chunk(frm,z2)
            wait_for(a,x_recv.at[d,i])
            ah=a.at[:,2*d:2*d+2]
            remote(ah,ah,f_send.at[d],f_recv.at[i],device(to,z,y,c)).start()
            remote(a,a,c_send.at[0],c_recv.at[0],device(x,z,y,1-c)).start()
    def last(i):
        z2=(z+8-order(i))%8
        a=chunk(far,z2)
        wait_for(a,f_recv.at[i])
        remote(a,a,c_send.at[0],c_recv.at[0],device(x,z,y,1-c)).start()
    def hand(s,first,count,unit,op):
        tile=unit//32; u=unit%32
        xo,co,t=owner(tile)
        src=qg_in.at[s,:,pl.ds(first,count)]; dst=qg.at[t,:,pl.ds(u,count)]
        @pl.when((xo!=x)|(co!=c))
        def _():
            cp=remote(src,dst,o_send.at[0],o_recv.at[0],device(xo,z,y,co))
            if op=="start": cp.start()
            else: cp.wait_send()
        if op=="start":
            @pl.when((xo==x)&(co==c))
            def _():
                pltpu.make_async_copy(src,dst,o_recv.at[0]).start()
    def spread(i,op):
        z2=(z+8-order(i))%8
        if op=="start":
            wait_for(qg_in.at[0:4],b_recv.at[i])
        def one(y2,_):
            s=z2*4+y2
            unit=(((x_lo*8+z2)*2+x_hi)*8+y2*2+c)*3
            @pl.when((unit%32)<=29)
            def _():
                hand(s,0,3,unit,op)
            @pl.when((unit%32)>29)
            def _():
                for e in range(3):
                    hand(s,e,1,unit+e,op)
            return 0
        lax.fori_loop(0,4,one,0)
    def loop(lo,hi,*acts):
        def body(i,_):
            for act in acts: act(i)
            return 0
        lax.fori_loop(lo,hi,body,0)
    def seq(lo,hi,*acts):
        loop(lo,hi,*[(lambda i,f=f,d=d: f(i+d)) for f,d in acts])
    def spread_start(i):
        spread(i,"start")
    fetch.wait()
    pick_kv(0)
    greeted()
    send_kv(0)
    loop(1,8,pick_kv,send_kv)
    wait_for(q_vm,ld.at[8]); wait_for(g_vm,ld.at[9])
    loop(0,8,pick_qg,send_qg)
    loop(0,4,ring)
    seq(4,8,(ring,0),(halves,-4))
    seq(4,8,(halves,0),(spread_start,-4))
    seq(0,4,(last,0),(spread_start,4))
    loop(4,8,last)
    wait_for(kv_out.at[0:31],a_send.at[0])
    wait_for(qg_out.at[0:31],b_send.at[0])
    loop(0,8,lambda i: spread(i,"done"))
    for d in range(2):
        wait_for(kv.at[:,0,:,0,:,0],x_send.at[d])
        wait_for(kv.at[:,0,:,0,0:2,0],f_send.at[d])
    wait_for(kv.at[:,:,:,:,:,0],c_send.at[0])
    wait_for(kv.at[:,:,:,:,:,0],c_recv.at[0])
    wait_for(qg,o_recv.at[0])

def gather(off,q,k,v,g):
    return pl.pallas_call(gather_kernel,
        out_shape=(pltpu.VMEM(KV,BF),pltpu.VMEM(QG,BF)),
        in_specs=[ANY]*5,
        out_specs=(VM,VM),
        scratch_shapes=[pltpu.VMEM((24,4,4096),BF)]*3+[pltpu.VMEM((3,8,4096),BF)]+[pltpu.VMEM((32,2,3,8,HD),BF)]*3+[
            pltpu.SMEM((HEADS,),jnp.int32),DMA((11,)),DMA((1,)),DMA((8,)),DMA((1,)),DMA((8,)),DMA((2,)),DMA((2,8)),DMA((2,)),DMA((8,)),DMA((1,)),DMA((1,)),DMA((1,)),DMA((1,))],
        name="gather",
        compiler_params=pltpu.CompilerParams(collective_id=0,has_side_effects=True,vmem_limit_bytes=40<<20))(*[afar(a) for a in (off,q,k,v,g)])

def scatter_kernel(dkv, og, out,
                   own, far_in, near_in, last_in, og_in, fin,
                   c_send, c_recv, g_send, g_recv, far_send, far_recv, near_send, last_send, fin_recv, p_send, p_recv):
    x_lo,z,x_hi,y,c=place()
    x=x_hi*2+x_lo
    right=(x+1)%4; left=(x+3)%4; far=(x+2)%4
    mine=z*4+y
    cols=pl.ds(pl.multiple_of(mine*HD,HD),HD)
    def at_z(i):
        return (z+order(7-i))%8
    greet(x,z,y,c)
    greeted()
    def back(op):
        def one(i,_):
            t=i//12; e=i%12
            blk=t*4+x+(t%2)*(3-2*x)
            tile=2*blk+(c+t)%2
            def hand(unit,count):
                piece=unit//3; k=unit%3; u=unit-tile*32
                xp=((piece//8)%2)*2+(piece//128)
                zp=(piece//16)%8; yp=(piece%8)//2; cp_=piece%2
                s=zp*4+yp
                src=og.at[t,:,pl.ds(u,count)]; dst=og_in.at[s,:,pl.ds(k,count)]
                sem=g_recv.at[zp]
                @pl.when((xp!=x)|(cp_!=c))
                def _():
                    cp=remote(src,dst,g_send.at[0],sem,device(xp,z,y,cp_))
                    if op=="start": cp.start()
                    else: cp.wait_send()
                if op=="start":
                    @pl.when((xp==x)&(cp_==c))
                    def _():
                        pltpu.make_async_copy(src,dst,sem).start()
            @pl.when(e<10)
            def _():
                hand(((tile*32+2)//3+e)*3,3)
            @pl.when(e>=10)
            def _():
                n=e-10; r=tile%3
                hand(tile*32+n+30*(1-(r+1)//2)+30*n*(r%2),1)
            return 0
        lax.fori_loop(0,36,one,0)
    for i in range(8):
        z2=at_z(i)
        remote(dkv.at[:,:,z2,:,:,1-c],own.at[:,:,z2],c_send.at[0],c_recv.at[i],device(x,z,y,1-c)).start()
    back("start")
    def to_rows(a, src, s, j):
        dst=out.at[2*a:2*a+2,:,:,cols]
        def away():
            remote(src,dst,p_send.at[a],p_recv.at[a],device(x,s//4,s%4,c)).start()
        if j:
            away()
        else:
            pl.when(s!=mine)(away)
            @pl.when(s==mine)
            def _():
                pltpu.make_async_copy(src,dst,p_recv.at[a]).start()
    def sum_cores(i):
        z2=at_z(i)
        wait_for(own.at[:,:,z2],c_recv.at[i])
        for xl in range(2):
            for xh in range(2):
                own[:,xl,z2,xh]=(own[:,xl,z2,xh].astype(F32)+dkv[:,xl,z2,xh,:,c].astype(F32)).astype(BF)
        ef=own.at[:,far%2,z2,far//2]
        remote(ef.at[:,0:2],far_in.at[0,z2],far_send.at[0],far_recv.at[0,i],device(right,z,y,c)).start()
        remote(ef.at[:,2:4],far_in.at[1,z2],far_send.at[0],far_recv.at[1,i],device(left,z,y,c)).start()
    def rows_back(i):
        z2=at_z(i)
        wait_for(og_in.at[0:4],g_recv.at[z2])
        for j in range(4):
            s=z2*4+(y+j)%4
            to_rows(0,og_in.at[s],s,j)
    def relay(i):
        z2=at_z(i)
        for d,peer in ((0,right),(1,left)):
            lo=2*d
            buf=far_in.at[d,z2]
            wait_for(buf,far_recv.at[d,i])
            far_in[d,z2]=(far_in[d,z2].astype(F32)+own[:,peer%2,z2,peer//2,lo:lo+2].astype(F32)).astype(BF)
            remote(buf,last_in.at[d,z2],last_send.at[0],fin_recv.at[i],device(peer,z,y,c)).start()
        er=own.at[:,right%2,z2,right//2]; el=own.at[:,left%2,z2,left//2]
        remote(er.at[:,2:4],near_in.at[0,z2],near_send.at[0],fin_recv.at[i],device(right,z,y,c)).start()
        remote(el.at[:,0:2],near_in.at[1,z2],near_send.at[0],fin_recv.at[i],device(left,z,y,c)).start()
    def finish(i):
        z2=at_z(i)
        wait_for(own.at[:,0,z2],fin_recv.at[i])
        for d in range(2):
            lo=2*d
            fin[:,pl.ds(z2*4+lo,2)]=(own[:,x_lo,z2,x_hi,lo:lo+2].astype(F32)+last_in[d,z2].astype(F32)+near_in[1-d,z2].astype(F32)).astype(BF)
        for j in range(4):
            s=z2*4+(y+j)%4
            to_rows(1,fin.at[:,s],s,j)
    def loop(lo,hi,*acts):
        def body(i,_):
            for act in acts: act(i)
            return 0
        lax.fori_loop(lo,hi,body,0)
    loop(0,8,sum_cores)
    loop(0,8,rows_back)
    loop(0,4,relay)
    loop(4,8,relay,lambda i: finish(i-4))
    loop(4,8,finish)
    back("done")
    wait_for(own,c_send.at[0])
    for b,sem in ((far_in,far_send),(near_in,near_send),(last_in,last_send)):
        wait_for(b,sem.at[0])
    wait_for(og_in.at[0:31],p_send.at[0])
    wait_for(fin.at[:,0:31],p_send.at[1])
    for a in range(2):
        wait_for(out.at[2*a:2*a+2],p_recv.at[a])

def scatter(dkv,og):
    return pl.pallas_call(scatter_kernel,
        out_shape=pltpu.VMEM((4,3,8,4096),BF),
        in_specs=[VM]*2,
        out_specs=VM,
        scratch_shapes=[pltpu.VMEM((2,2,8,2,4,3,8,HD),BF)]+[pltpu.VMEM((2,8,2,2,3,8,HD),BF)]*3+[pltpu.VMEM((32,2,3,8,HD),BF),pltpu.VMEM((2,32,3,8,HD),BF),
            DMA((1,)),DMA((8,)),DMA((1,)),DMA((8,)),DMA((1,)),DMA((2,8)),DMA((1,)),DMA((1,)),DMA((8,)),DMA((2,)),DMA((2,))],
        name="scatter",
        compiler_params=pltpu.CompilerParams(collective_id=1,has_side_effects=True,vmem_limit_bytes=40<<20))(held(dkv),held(og))

def settle_kernel(src,*refs):
    cps=[pltpu.make_async_copy(src.at[i],refs[i],refs[4].at[i]) for i in range(4)]
    for cp in cps: cp.start()
    for cp in cps: cp.wait()

def settle(out):
    return pl.pallas_call(settle_kernel,
        out_shape=(jax.ShapeDtypeStruct((3,8,4096),BF),)*4,
        in_specs=[VM],out_specs=(ANY,)*4,
        scratch_shapes=[DMA((4,))],
        name="settle",
        compiler_params=pltpu.CompilerParams(vmem_limit_bytes=40<<20))(held(out))

def on_device(queries,key_states,value_states,out_grad,offsets,block_mask):
    kv,qg=gather(offsets,queries,key_states,value_states,out_grad.reshape(3,8,4096))
    dkv,og=attend(block_mask,kv,qg)
    outs=settle(scatter(dkv,og))
    return tuple(o.reshape(24,4096) for o in outs)


def solution(mesh):
    rows3=P(("ctx","head"),None,None); rows2=P(("ctx","head"),None)
    return jax.shard_map(on_device,mesh=mesh,in_specs=(rows3,rows3,rows3,rows2,P(),P()),
                         out_specs=(rows2,)*4,check_vma=False)
```

```python
import functools, jax, jax.numpy as jnp
from jax.sharding import PartitionSpec as P
from jax import lax
from jax.experimental import pallas as pl
from jax.experimental.pallas import tpu as pltpu
BF=jnp.bfloat16; F32=jnp.float32
HEADS=32; NB=12; BLK=512; TQ=256; HD=128
SCALE=HD**-0.5
C2=SCALE*1.4426950408889634
FU=4; GB=4

def dot(a,b):
    return jnp.dot(a,b,preferred_element_type=F32)

def dot_t(a,b):
    return lax.dot_general(a,b,(((0,),(0,)),((),())),preferred_element_type=F32)

def my_tiles():
    ctx=lax.axis_index("ctx"); hd=lax.axis_index("head")
    return (hd//8)*2+ctx//8, hd%2

def attend_kernel(mask_hbm, kv_ref, qg_ref, dkv_ref, og_ref,
                  p_sc, m_sc, dk_acc, dv_acc, ot_acc, dqt_acc, s_sc, live, mask_ref, ld):
    grp,core=my_tiles()
    fetch=pltpu.make_async_copy(mask_hbm,mask_ref,ld.at[0])
    fetch.start()
    kv_rows=kv_ref.reshape(2,768,8,HD)
    dkv_rows=dkv_ref.reshape(2,768,8,HD)
    def blk(i,j):
        return kv_rows[i,pl.ds(pl.multiple_of(j*64,64),64)].reshape(BLK,HD)
    @pl.loop(0,NB)
    def _(j):
        z=jnp.zeros((BLK,HD),F32)
        rows=pl.ds(pl.multiple_of(j*BLK,BLK),BLK)
        dk_acc[rows]=z; dv_acc[rows]=z
    def tile(t):
        bm=grp
        b=t*4+bm+(t%2)*(3-2*bm)
        half=(core+t)%2
        q=qg_ref[t,0].reshape(TQ,HD); g=qg_ref[t,1].reshape(TQ,HD)
        qt=q.T; gt=g.T
        def count(j,n):
            live[n]=j
            return n+mask_ref[b,j]
        live[0]=b
        n_live=lax.fori_loop(0,b,count,1)
        live[n_live]=b
        s=dot(blk(0,b),qt)
        kr=lax.broadcasted_iota(jnp.int32,(BLK,TQ),0); qc=lax.broadcasted_iota(jnp.int32,(BLK,TQ),1)+half*TQ
        s=jnp.where(kr<=qc,s,-1e30)
        s_sc[0]=s
        def fwd(i,cur,carry):
            m_old,l,m=carry
            s_next=dot(blk(0,live[i+1]),qt)
            s_sc[1-cur]=s_next
            m_next=jnp.maximum(m,jnp.max(s_next,axis=0,keepdims=True))
            mc=m*C2
            alpha=jnp.exp2(m_old*C2-mc)
            p=jnp.exp2(s_sc[cur]*C2-mc)
            pb=p.astype(BF)
            p_sc[i]=pb
            m_sc[i]=m
            l=l*alpha+jnp.sum(p,axis=0,keepdims=True)
            ot_acc[...]=ot_acc[...]*alpha+dot_t(blk(1,live[i]),pb)
            return m,l,m_next
        ot_acc[...]=jnp.zeros((HD,TQ),F32)
        m=jnp.max(s,axis=0,keepdims=True)
        c=(m,jnp.zeros((1,TQ),F32),m)
        def groups(step,size,c):
            start=0
            while size:
                count=(n_live-start)//size
                def run(i,c,start=start,size=size):
                    return step(start+i*size,size,c)
                c=lax.fori_loop(0,count,run,c)
                start=start+count*size
                size//=2
            return c
        def fwds(i,size,c):
            for e in range(size): c=fwd(i+e,e%2,c)
            return c
        m,l,_=groups(fwds,FU,c)
        inv=1.0/l
        ot=(ot_acc[...]*inv).astype(BF)
        og_ref[t,0]=ot.T.reshape(32,8,HD)
        r=jnp.sum(gt.astype(F32)*ot.astype(F32),axis=0,keepdims=True)
        mc=m*C2
        def bwd(js,slots,c):
            acc=dqt_acc[...]
            for j,slot in zip(js,slots):
                f=jnp.exp2(m_sc[slot]*C2-mc)*inv
                p=p_sc[slot].astype(F32)*f
                dp=dot(blk(1,j),gt)
                ds=(p*(dp-r)).astype(BF)
                rows=pl.ds(pl.multiple_of(j*BLK,BLK),BLK)
                dv_acc[rows]+=dot(p.astype(BF),g)
                dk_acc[rows]+=dot(ds,q)
                acc=acc+dot_t(blk(0,j),ds)
            dqt_acc[...]=acc
            return c
        dqt_acc[...]=jnp.zeros((HD,TQ),F32)
        def bwds(i,size,c):
            idx=[i+e for e in range(size)]
            return bwd([live[e] for e in idx],idx,c)
        groups(bwds,GB,0)
        og_ref[t,1]=(dqt_acc[...]*SCALE).astype(BF).T.reshape(32,8,HD)
    def settle_blocks(lo,hi):
        @pl.loop(lo,hi)
        def _(j):
            rows=pl.ds(pl.multiple_of(j*BLK,BLK),BLK)
            un=pl.ds(pl.multiple_of(j*64,64),64)
            dkv_rows[0,un]=(dk_acc[rows]*SCALE).astype(BF).reshape(64,8,HD)
            dkv_rows[1,un]=dv_acc[rows].astype(BF).reshape(64,8,HD)
    fetch.wait()
    @pl.loop(0,3)
    def _(t):
        tile(t)
    settle_blocks(0,NB)

KV=(2,2,8,2,4,2,3,8,HD)
QG=(3,2,32,8,HD)
VM=pl.BlockSpec(memory_space=pltpu.VMEM)
ANY=pl.BlockSpec(memory_space=pl.ANY)
DMA=pltpu.SemaphoreType.DMA
def held(x):
    return pltpu.with_memory_space_constraint(x,pltpu.VMEM)
def afar(x):
    return pltpu.with_memory_space_constraint(x,pltpu.HBM)
def attend(mask,kv,qg):
    return pl.pallas_call(attend_kernel,
        out_shape=(pltpu.VMEM(KV,BF),pltpu.VMEM(QG,BF)),
        in_specs=[ANY,VM,VM],
        out_specs=(VM,VM),
        scratch_shapes=[
            pltpu.VMEM((NB,BLK,TQ),BF),pltpu.VMEM((NB,1,TQ),F32),pltpu.VMEM((NB*BLK,HD),F32),pltpu.VMEM((NB*BLK,HD),F32),
            pltpu.VMEM((HD,TQ),F32),pltpu.VMEM((HD,TQ),F32),pltpu.VMEM((2,BLK,TQ),F32),pltpu.SMEM((16,),jnp.int32),pltpu.SMEM((NB,NB),jnp.int32),DMA((1,))],
        name="attend",
        compiler_params=pltpu.CompilerParams(vmem_limit_bytes=40<<20))(afar(mask),held(kv),held(qg))

MESH=pl.DeviceIdType.MESH

def place():
    ctx=lax.axis_index("ctx"); hd=lax.axis_index("head")
    return ctx//8, ctx%8, hd//8, (hd%8)//2, hd%2

def device(x, z, y, c):
    return ((x%2)*8+z, (x//2)*8+y*2+c)

def owner(tile):
    blk=tile//2; t=blk//4; bm=blk%4
    return bm+(t%2)*(3-2*bm), (tile%2+t)%2, t

def order(i):
    return (i%2)*((i+1)//2)+(1-i%2)*((8-i//2)%8)

def remote(src, dst, send, recv, dev):
    return pltpu.make_async_remote_copy(src_ref=src, dst_ref=dst, send_sem=send, recv_sem=recv,
                                        device_id=dev, device_id_type=MESH)

def wait_for(ref, sem):
    pltpu.make_async_copy(ref,ref,sem).wait()

def greet(x, z, y, c):
    barrier=pltpu.get_barrier_semaphore()
    def plane(i,_):
        s=(z*4+y+i)%32
        pl.semaphore_signal(barrier, inc=1, device_id=device(x,s//4,s%4,c), device_id_type=MESH)
        return 0
    lax.fori_loop(1,32,plane,0,unroll=True)
    for i in range(1,8):
        s=(x*2+c+i)%8
        pl.semaphore_signal(barrier, inc=1, device_id=device(s//2,z,y,s%2), device_id_type=MESH)

def greeted():
    pl.semaphore_wait(pltpu.get_barrier_semaphore(), 38)

def gather_kernel(off_hbm, q, k, v, g, kv, qg, q_vm, k_vm, v_vm, g_vm, kv_out, qg_out, qg_in,
                  off, ld, a_send, a_recv, b_send, b_recv, x_send, x_recv, f_send, f_recv, c_send, c_recv, o_send, o_recv):
    x_lo,z,x_hi,y,c=place()
    x=x_hi*2+x_lo
    right=(x+1)%4; left=(x+3)%4; far=(x+2)%4
    mine=z*4+y
    for i in range(8):
        cols=pl.ds(pl.multiple_of(((z+order(i))%8)*512,512),512)
        pltpu.make_async_copy(k.at[:,:,cols],k_vm.at[:,:,cols],ld.at[i]).start()
        pltpu.make_async_copy(v.at[:,:,cols],v_vm.at[:,:,cols],ld.at[i]).start()
    pltpu.make_async_copy(q,q_vm,ld.at[8]).start()
    pltpu.make_async_copy(g,g_vm,ld.at[9]).start()
    fetch=pltpu.make_async_copy(off_hbm,off,ld.at[10])
    fetch.start()
    greet(x,z,y,c)
    row=lax.broadcasted_iota(jnp.int32,(24,96),0); col=lax.broadcasted_iota(jnp.int32,(24,96),1)
    lead=col-row*4
    def columns(h):
        return pl.ds(pl.multiple_of(h*HD,HD),HD)
    def pick(ref,h,hot):
        return dot(hot,ref[:,:,columns(h)].reshape(96,HD)).reshape(3,8,HD).astype(BF)
    def hot_of(h):
        return (lead==off[h]).astype(F32).astype(BF)
    def chunk(x2,z2):
        return kv.at[:,x2%2,z2,x2//2,:,c]
    def pick_kv(i):
        wait_for(k_vm.at[:,:,pl.ds(0,1024)],ld.at[i])
        z2=(z+order(i))%8
        for j in range(4):
            h=z2*4+(y+j)%4
            hot=hot_of(h)
            kv_out[h,0]=pick(k_vm,h,hot)
            kv_out[h,1]=pick(v_vm,h,hot)
    def pick_qg(i):
        z2=(z+order(i))%8
        for j in range(4):
            h=z2*4+(y+j)%4
            qg_out[h,0]=pick(q_vm,h,hot_of(h))
            qg_out[h,1]=g_vm[:,:,columns(h)]
    def to_plane(i, out, dst, send, recv):
        z2=(z+order(i))%8
        for j in range(4):
            y2=(y+j)%4
            src=out.at[z2*4+y2]
            if j:
                remote(src,dst,send,recv,device(x,z2,y2,c)).start()
            else:
                @pl.when(z2!=z)
                def _():
                    remote(src,dst,send,recv,device(x,z2,y2,c)).start()
                @pl.when(z2==z)
                def _():
                    pltpu.make_async_copy(src,dst,recv).start()
    def send_kv(i):
        to_plane(i,kv_out,kv.at[:,x_lo,z,x_hi,y,c],a_send.at[0],a_recv.at[i])
    def send_qg(i):
        to_plane(i,qg_out,qg_in.at[mine],b_send.at[0],b_recv.at[i])
    def ring(i):
        z2=(z+8-order(i))%8
        wait_for(kv_out.at[0:4],a_recv.at[i])
        own=chunk(x,z2)
        remote(own,own,x_send.at[0],x_recv.at[0,i],device(right,z,y,c)).start()
        remote(own,own,x_send.at[1],x_recv.at[1,i],device(left,z,y,c)).start()
        remote(own,own,c_send.at[0],c_recv.at[0],device(x,z,y,1-c)).start()
    def halves(i):
        z2=(z+8-order(i))%8
        for d,frm,to in ((0,left,right),(1,right,left)):
            a=chunk(frm,z2)
            wait_for(a,x_recv.at[d,i])
            ah=a.at[:,2*d:2*d+2]
            remote(ah,ah,f_send.at[d],f_recv.at[i],device(to,z,y,c)).start()
            remote(a,a,c_send.at[0],c_recv.at[0],device(x,z,y,1-c)).start()
    def last(i):
        z2=(z+8-order(i))%8
        a=chunk(far,z2)
        wait_for(a,f_recv.at[i])
        remote(a,a,c_send.at[0],c_recv.at[0],device(x,z,y,1-c)).start()
    def hand(s,first,count,unit,op):
        tile=unit//32; u=unit%32
        xo,co,t=owner(tile)
        src=qg_in.at[s,:,pl.ds(first,count)]; dst=qg.at[t,:,pl.ds(u,count)]
        @pl.when((xo!=x)|(co!=c))
        def _():
            cp=remote(src,dst,o_send.at[0],o_recv.at[0],device(xo,z,y,co))
            if op=="start": cp.start()
            else: cp.wait_send()
        if op=="start":
            @pl.when((xo==x)&(co==c))
            def _():
                pltpu.make_async_copy(src,dst,o_recv.at[0]).start()
    def spread(i,op):
        z2=(z+8-order(i))%8
        if op=="start":
            wait_for(qg_in.at[0:4],b_recv.at[i])
        def one(y2,_):
            s=z2*4+y2
            unit=(((x_lo*8+z2)*2+x_hi)*8+y2*2+c)*3
            @pl.when((unit%32)<=29)
            def _():
                hand(s,0,3,unit,op)
            @pl.when((unit%32)>29)
            def _():
                for e in range(3):
                    hand(s,e,1,unit+e,op)
            return 0
        lax.fori_loop(0,4,one,0)
    def loop(lo,hi,*acts):
        def body(i,_):
            for act in acts: act(i)
            return 0
        lax.fori_loop(lo,hi,body,0)
    def seq(lo,hi,*acts):
        loop(lo,hi,*[(lambda i,f=f,d=d: f(i+d)) for f,d in acts])
    def spread_start(i):
        spread(i,"start")
    fetch.wait()
    pick_kv(0)
    greeted()
    send_kv(0)
    loop(1,8,pick_kv,send_kv)
    wait_for(q_vm,ld.at[8]); wait_for(g_vm,ld.at[9])
    loop(0,8,pick_qg,send_qg)
    loop(0,4,ring)
    seq(4,8,(ring,0),(halves,-4))
    seq(4,8,(halves,0),(spread_start,-4))
    seq(0,4,(last,0),(spread_start,4))
    loop(4,8,last)
    wait_for(kv_out.at[0:31],a_send.at[0])
    wait_for(qg_out.at[0:31],b_send.at[0])
    loop(0,8,lambda i: spread(i,"done"))
    for d in range(2):
        wait_for(kv.at[:,0,:,0,:,0],x_send.at[d])
        wait_for(kv.at[:,0,:,0,0:2,0],f_send.at[d])
    wait_for(kv.at[:,:,:,:,:,0],c_send.at[0])
    wait_for(kv.at[:,:,:,:,:,0],c_recv.at[0])
    wait_for(qg,o_recv.at[0])

def gather(off,q,k,v,g):
    return pl.pallas_call(gather_kernel,
        out_shape=(pltpu.VMEM(KV,BF),pltpu.VMEM(QG,BF)),
        in_specs=[ANY]*5,
        out_specs=(VM,VM),
        scratch_shapes=[pltpu.VMEM((24,4,4096),BF)]*3+[pltpu.VMEM((3,8,4096),BF)]+[pltpu.VMEM((32,2,3,8,HD),BF)]*3+[
            pltpu.SMEM((HEADS,),jnp.int32),DMA((11,)),DMA((1,)),DMA((8,)),DMA((1,)),DMA((8,)),DMA((2,)),DMA((2,8)),DMA((2,)),DMA((8,)),DMA((1,)),DMA((1,)),DMA((1,)),DMA((1,))],
        name="gather",
        compiler_params=pltpu.CompilerParams(collective_id=0,has_side_effects=True,vmem_limit_bytes=40<<20))(*[afar(a) for a in (off,q,k,v,g)])

def scatter_kernel(dkv, og, out,
                   own, far_in, near_in, last_in, og_in, fin,
                   c_send, c_recv, g_send, g_recv, far_send, far_recv, near_send, last_send, fin_recv, p_send, p_recv):
    x_lo,z,x_hi,y,c=place()
    x=x_hi*2+x_lo
    right=(x+1)%4; left=(x+3)%4; far=(x+2)%4
    mine=z*4+y
    cols=pl.ds(pl.multiple_of(mine*HD,HD),HD)
    def at_z(i):
        return (z+order(7-i))%8
    greet(x,z,y,c)
    greeted()
    def back(op):
        def one(i,_):
            t=i//12; e=i%12
            blk=t*4+x+(t%2)*(3-2*x)
            tile=2*blk+(c+t)%2
            def hand(unit,count):
                piece=unit//3; k=unit%3; u=unit-tile*32
                xp=((piece//8)%2)*2+(piece//128)
                zp=(piece//16)%8; yp=(piece%8)//2; cp_=piece%2
                s=zp*4+yp
                src=og.at[t,:,pl.ds(u,count)]; dst=og_in.at[s,:,pl.ds(k,count)]
                sem=g_recv.at[zp]
                @pl.when((xp!=x)|(cp_!=c))
                def _():
                    cp=remote(src,dst,g_send.at[0],sem,device(xp,z,y,cp_))
                    if op=="start": cp.start()
                    else: cp.wait_send()
                if op=="start":
                    @pl.when((xp==x)&(cp_==c))
                    def _():
                        pltpu.make_async_copy(src,dst,sem).start()
            @pl.when(e<10)
            def _():
                hand(((tile*32+2)//3+e)*3,3)
            @pl.when(e>=10)
            def _():
                n=e-10; r=tile%3
                hand(tile*32+n+30*(1-(r+1)//2)+30*n*(r%2),1)
            return 0
        lax.fori_loop(0,36,one,0)
    for i in range(8):
        z2=at_z(i)
        remote(dkv.at[:,:,z2,:,:,1-c],own.at[:,:,z2],c_send.at[0],c_recv.at[i],device(x,z,y,1-c)).start()
    back("start")
    def to_rows(a, src, s, j):
        dst=out.at[2*a:2*a+2,:,:,cols]
        def away():
            remote(src,dst,p_send.at[a],p_recv.at[a],device(x,s//4,s%4,c)).start()
        if j:
            away()
        else:
            pl.when(s!=mine)(away)
            @pl.when(s==mine)
            def _():
                pltpu.make_async_copy(src,dst,p_recv.at[a]).start()
    def sum_cores(i):
        z2=at_z(i)
        wait_for(own.at[:,:,z2],c_recv.at[i])
        for xl in range(2):
            for xh in range(2):
                own[:,xl,z2,xh]=(own[:,xl,z2,xh].astype(F32)+dkv[:,xl,z2,xh,:,c].astype(F32)).astype(BF)
        ef=own.at[:,far%2,z2,far//2]
        remote(ef.at[:,0:2],far_in.at[0,z2],far_send.at[0],far_recv.at[0,i],device(right,z,y,c)).start()
        remote(ef.at[:,2:4],far_in.at[1,z2],far_send.at[0],far_recv.at[1,i],device(left,z,y,c)).start()
    def rows_back(i):
        z2=at_z(i)
        wait_for(og_in.at[0:4],g_recv.at[z2])
        for j in range(4):
            s=z2*4+(y+j)%4
            to_rows(0,og_in.at[s],s,j)
    def relay(i):
        z2=at_z(i)
        for d,peer in ((0,right),(1,left)):
            lo=2*d
            buf=far_in.at[d,z2]
            wait_for(buf,far_recv.at[d,i])
            far_in[d,z2]=(far_in[d,z2].astype(F32)+own[:,peer%2,z2,peer//2,lo:lo+2].astype(F32)).astype(BF)
            remote(buf,last_in.at[d,z2],last_send.at[0],fin_recv.at[i],device(peer,z,y,c)).start()
        er=own.at[:,right%2,z2,right//2]; el=own.at[:,left%2,z2,left//2]
        remote(er.at[:,2:4],near_in.at[0,z2],near_send.at[0],fin_recv.at[i],device(right,z,y,c)).start()
        remote(el.at[:,0:2],near_in.at[1,z2],near_send.at[0],fin_recv.at[i],device(left,z,y,c)).start()
    def finish(i):
        z2=at_z(i)
        wait_for(own.at[:,0,z2],fin_recv.at[i])
        for d in range(2):
            lo=2*d
            fin[:,pl.ds(z2*4+lo,2)]=(own[:,x_lo,z2,x_hi,lo:lo+2].astype(F32)+last_in[d,z2].astype(F32)+near_in[1-d,z2].astype(F32)).astype(BF)
        for j in range(4):
            s=z2*4+(y+j)%4
            to_rows(1,fin.at[:,s],s,j)
    def loop(lo,hi,*acts):
        def body(i,_):
            for act in acts: act(i)
            return 0
        lax.fori_loop(lo,hi,body,0)
    loop(0,8,sum_cores)
    loop(0,8,rows_back)
    loop(0,4,relay)
    loop(4,8,relay,lambda i: finish(i-4))
    loop(4,8,finish)
    back("done")
    wait_for(own,c_send.at[0])
    for b,sem in ((far_in,far_send),(near_in,near_send),(last_in,last_send)):
        wait_for(b,sem.at[0])
    wait_for(og_in.at[0:31],p_send.at[0])
    wait_for(fin.at[:,0:31],p_send.at[1])
    for a in range(2):
        wait_for(out.at[2*a:2*a+2],p_recv.at[a])

def scatter(dkv,og):
    return pl.pallas_call(scatter_kernel,
        out_shape=pltpu.VMEM((4,3,8,4096),BF),
        in_specs=[VM]*2,
        out_specs=VM,
        scratch_shapes=[pltpu.VMEM((2,2,8,2,4,3,8,HD),BF)]+[pltpu.VMEM((2,8,2,2,3,8,HD),BF)]*3+[pltpu.VMEM((32,2,3,8,HD),BF),pltpu.VMEM((2,32,3,8,HD),BF),
            DMA((1,)),DMA((8,)),DMA((1,)),DMA((8,)),DMA((1,)),DMA((2,8)),DMA((1,)),DMA((1,)),DMA((8,)),DMA((2,)),DMA((2,))],
        name="scatter",
        compiler_params=pltpu.CompilerParams(collective_id=1,has_side_effects=True,vmem_limit_bytes=40<<20))(held(dkv),held(og))

def settle_kernel(src,*refs):
    cps=[pltpu.make_async_copy(src.at[i],refs[i],refs[4].at[i]) for i in range(4)]
    for cp in cps: cp.start()
    for cp in cps: cp.wait()

def settle(out):
    return pl.pallas_call(settle_kernel,
        out_shape=(jax.ShapeDtypeStruct((3,8,4096),BF),)*4,
        in_specs=[VM],out_specs=(ANY,)*4,
        scratch_shapes=[DMA((4,))],
        name="settle",
        compiler_params=pltpu.CompilerParams(vmem_limit_bytes=40<<20))(held(out))

def on_device(queries,key_states,value_states,out_grad,offsets,block_mask):
    kv,qg=gather(offsets,queries,key_states,value_states,out_grad.reshape(3,8,4096))
    dkv,og=attend(block_mask,kv,qg)
    outs=settle(scatter(dkv,og))
    return tuple(o.reshape(24,4096) for o in outs)


def solution(mesh):
    rows3=P(("ctx","head"),None,None); rows2=P(("ctx","head"),None)
    return jax.shard_map(on_device,mesh=mesh,in_specs=(rows3,rows3,rows3,rows2,P(),P()),
                         out_specs=(rows2,)*4,check_vma=False)
```

```python
import functools, jax, jax.numpy as jnp
from jax.sharding import PartitionSpec as P
from jax import lax
from jax.experimental import pallas as pl
from jax.experimental.pallas import tpu as pltpu
BF=jnp.bfloat16; F32=jnp.float32
HEADS=32; NB=12; BLK=512; TQ=256; HD=128
SCALE=HD**-0.5
C2=SCALE*1.4426950408889634
FU=4; GB=4

def dot(a,b):
    return jnp.dot(a,b,preferred_element_type=F32)

def dot_t(a,b):
    return lax.dot_general(a,b,(((0,),(0,)),((),())),preferred_element_type=F32)

def my_tiles():
    ctx=lax.axis_index("ctx"); hd=lax.axis_index("head")
    return (hd//8)*2+ctx//8, hd%2

def attend_kernel(mask_hbm, kv_ref, qg_ref, dkv_ref, og_ref,
                  p_sc, m_sc, dk_acc, dv_acc, ot_acc, dqt_acc, s_sc, qt_sc, gt_sc, st_sc, live, pair_tile, mask_ref, ld):
    grp,core=my_tiles()
    fetch=pltpu.make_async_copy(mask_hbm,mask_ref,ld.at[0])
    fetch.start()
    kv_rows=kv_ref.reshape(2,768,8,HD)
    dkv_rows=dkv_ref.reshape(2,768,8,HD)
    def blk(i,j):
        return kv_rows[i,pl.ds(pl.multiple_of(j*64,64),64)].reshape(BLK,HD)
    @pl.loop(0,NB)
    def _(j):
        z=jnp.zeros((BLK,HD),F32)
        rows=pl.ds(pl.multiple_of(j*BLK,BLK),BLK)
        dk_acc[rows]=z; dv_acc[rows]=z
    def groups(first,n_live,step,size,c):
        start=first
        while size:
            count=(n_live-start)//size
            def run(i,c,start=start,size=size):
                return step(start+i*size,size,c)
            c=lax.fori_loop(0,count,run,c)
            start=start+count*size
            size//=2
        return c
    def tile_of(t):
        return t*4+grp+(t%2)*(3-2*grp), (core+t)%2
    def note(n,t,j):
        live[n]=j
        pair_tile[n]=t
    def list_blocks(t,n):
        def one(j,n):
            note(n,t,j)
            return n+mask_ref[tile_of(t)[0],j]
        return lax.fori_loop(0,tile_of(t)[0],one,n)
    def exps(t,slot,s,m_old,m):
        mc=m*C2
        alpha=jnp.exp2(m_old*C2-mc)
        p=jnp.exp2(s*C2-mc)
        pb=p.astype(BF)
        p_sc[slot]=pb
        m_sc[slot]=m
        return alpha,jnp.sum(p,axis=0,keepdims=True),pb
    def diagonals():
        for t in range(3):
            qt_sc[t]=qg_ref[t,0].reshape(TQ,HD).T
            gt_sc[t]=qg_ref[t,1].reshape(TQ,HD).T
        for t in range(3):
            b,half=tile_of(t)
            s=dot(blk(0,b),qt_sc[t])
            kr=lax.broadcasted_iota(jnp.int32,(BLK,TQ),0); qc=lax.broadcasted_iota(jnp.int32,(BLK,TQ),1)+half*TQ
            s=jnp.where(kr<=qc,s,-1e30)
            m=jnp.max(s,axis=0,keepdims=True)
            _,l,pb=exps(t,t,s,m,m)
            st_sc[t,0]=m; st_sc[t,1]=l; st_sc[t,2]=m
            ot_acc[t]=dot_t(blk(1,b),pb)
    def ahead(i,slot):
        t=pair_tile[i]
        s=dot(blk(0,live[i]),qt_sc[t])
        s_sc[slot]=s
        m=jnp.maximum(st_sc[t,2],jnp.max(s,axis=0,keepdims=True))
        st_sc[t,2]=m
        return m
    def fwd(i,cur,m):
        m_next=ahead(i+1,1-cur)
        t=pair_tile[i]
        alpha,total,pb=exps(t,i,s_sc[cur],st_sc[t,0],m)
        st_sc[t,0]=m
        st_sc[t,1]=st_sc[t,1]*alpha+total
        ot_acc[t]=ot_acc[t]*alpha+dot_t(blk(1,live[i]),pb)
        return m_next
    def fwds(i,size,m):
        for e in range(size): m=fwd(i+e,(e+1)%2,m)
        return m
    def finish():
        for t in range(3):
            inv=1.0/st_sc[t,1]
            ot=(ot_acc[t]*inv).astype(BF)
            og_ref[t,0]=ot.T.reshape(32,8,HD)
            st_sc[t,0]=st_sc[t,0]*C2
            st_sc[t,1]=inv
            st_sc[t,2]=jnp.sum(gt_sc[t].astype(F32)*ot.astype(F32),axis=0,keepdims=True)
            dqt_acc[t]=jnp.zeros((HD,TQ),F32)
    def bwd(i,size,c):
        for e in range(size):
            slot=i+e; j=live[slot]; t=pair_tile[slot]
            gt=gt_sc[t]; q=qg_ref[t,0].reshape(TQ,HD); g=qg_ref[t,1].reshape(TQ,HD)
            f=jnp.exp2(m_sc[slot]*C2-st_sc[t,0])*st_sc[t,1]
            p=p_sc[slot].astype(F32)*f
            dp=dot(blk(1,j),gt)
            ds=(p*(dp-st_sc[t,2])).astype(BF)
            rows=pl.ds(pl.multiple_of(j*BLK,BLK),BLK)
            dv_acc[rows]+=dot(p.astype(BF),g)
            dk_acc[rows]+=dot(ds,q)
            dqt_acc[t]+=dot_t(blk(0,j),ds)
        return c
    def settle_blocks(lo,hi):
        @pl.loop(lo,hi)
        def _(j):
            rows=pl.ds(pl.multiple_of(j*BLK,BLK),BLK)
            un=pl.ds(pl.multiple_of(j*64,64),64)
            dkv_rows[0,un]=(dk_acc[rows]*SCALE).astype(BF).reshape(64,8,HD)
            dkv_rows[1,un]=dv_acc[rows].astype(BF).reshape(64,8,HD)
    diagonals()
    fetch.wait()
    for t in range(3): note(t,t,tile_of(t)[0])
    pairs=3
    for t in range(3): pairs=list_blocks(t,pairs)
    note(pairs,0,0)
    groups(3,pairs,fwds,FU,ahead(3,1))
    finish()
    groups(0,pairs,bwd,GB,0)
    for t in range(3):
        og_ref[t,1]=(dqt_acc[t]*SCALE).astype(BF).T.reshape(32,8,HD)
    settle_blocks(0,NB)

KV=(2,2,8,2,4,2,3,8,HD)
QG=(3,2,32,8,HD)
VM=pl.BlockSpec(memory_space=pltpu.VMEM)
ANY=pl.BlockSpec(memory_space=pl.ANY)
DMA=pltpu.SemaphoreType.DMA
def held(x):
    return pltpu.with_memory_space_constraint(x,pltpu.VMEM)
def afar(x):
    return pltpu.with_memory_space_constraint(x,pltpu.HBM)
def attend(mask,kv,qg):
    return pl.pallas_call(attend_kernel,
        out_shape=(pltpu.VMEM(KV,BF),pltpu.VMEM(QG,BF)),
        in_specs=[ANY,VM,VM],
        out_specs=(VM,VM),
        scratch_shapes=[
            pltpu.VMEM((3*NB,BLK,TQ),BF),pltpu.VMEM((3*NB,1,TQ),F32),pltpu.VMEM((NB*BLK,HD),F32),pltpu.VMEM((NB*BLK,HD),F32),
            pltpu.VMEM((3,HD,TQ),F32),pltpu.VMEM((3,HD,TQ),F32),pltpu.VMEM((2,BLK,TQ),F32),pltpu.VMEM((3,HD,TQ),BF),pltpu.VMEM((3,HD,TQ),BF),pltpu.VMEM((3,3,1,TQ),F32),pltpu.SMEM((3*NB+1,),jnp.int32),pltpu.SMEM((3*NB+1,),jnp.int32),pltpu.SMEM((NB,NB),jnp.int32),DMA((1,))],
        name="attend",
        compiler_params=pltpu.CompilerParams(vmem_limit_bytes=40<<20))(afar(mask),held(kv),held(qg))

MESH=pl.DeviceIdType.MESH

def place():
    ctx=lax.axis_index("ctx"); hd=lax.axis_index("head")
    return ctx//8, ctx%8, hd//8, (hd%8)//2, hd%2

def device(x, z, y, c):
    return ((x%2)*8+z, (x//2)*8+y*2+c)

def owner(tile):
    blk=tile//2; t=blk//4; bm=blk%4
    return bm+(t%2)*(3-2*bm), (tile%2+t)%2, t

def order(i):
    return (i%2)*((i+1)//2)+(1-i%2)*((8-i//2)%8)

def remote(src, dst, send, recv, dev):
    return pltpu.make_async_remote_copy(src_ref=src, dst_ref=dst, send_sem=send, recv_sem=recv,
                                        device_id=dev, device_id_type=MESH)

def wait_for(ref, sem):
    pltpu.make_async_copy(ref,ref,sem).wait()

def greet(x, z, y, c):
    barrier=pltpu.get_barrier_semaphore()
    def plane(i,_):
        s=(z*4+y+i)%32
        pl.semaphore_signal(barrier, inc=1, device_id=device(x,s//4,s%4,c), device_id_type=MESH)
        return 0
    lax.fori_loop(1,32,plane,0,unroll=True)
    for i in range(1,8):
        s=(x*2+c+i)%8
        pl.semaphore_signal(barrier, inc=1, device_id=device(s//2,z,y,s%2), device_id_type=MESH)

def greeted():
    pl.semaphore_wait(pltpu.get_barrier_semaphore(), 38)

def gather_kernel(off_hbm, q, k, v, g, kv, qg, q_vm, k_vm, v_vm, g_vm, kv_out, qg_out, qg_in,
                  off, ld, a_send, a_recv, b_send, b_recv, x_send, x_recv, f_send, f_recv, c_send, c_recv, o_send, o_recv):
    x_lo,z,x_hi,y,c=place()
    x=x_hi*2+x_lo
    right=(x+1)%4; left=(x+3)%4; far=(x+2)%4
    mine=z*4+y
    greet(x,z,y,c)
    for i in range(8):
        cols=pl.ds(pl.multiple_of(((z+order(i))%8)*512,512),512)
        pltpu.make_async_copy(k.at[:,:,cols],k_vm.at[:,:,cols],ld.at[i]).start()
        pltpu.make_async_copy(v.at[:,:,cols],v_vm.at[:,:,cols],ld.at[i]).start()
    pltpu.make_async_copy(q,q_vm,ld.at[8]).start()
    pltpu.make_async_copy(g,g_vm,ld.at[9]).start()
    fetch=pltpu.make_async_copy(off_hbm,off,ld.at[10])
    fetch.start()
    row=lax.broadcasted_iota(jnp.int32,(24,96),0); col=lax.broadcasted_iota(jnp.int32,(24,96),1)
    lead=col-row*4
    def columns(h):
        return pl.ds(pl.multiple_of(h*HD,HD),HD)
    def pick(ref,h,hot):
        return dot(hot,ref[:,:,columns(h)].reshape(96,HD)).reshape(3,8,HD).astype(BF)
    def hot_of(h):
        return (lead==off[h]).astype(F32).astype(BF)
    def chunk(x2,z2):
        return kv.at[:,x2%2,z2,x2//2,:,c]
    def pick_kv(i):
        wait_for(k_vm.at[:,:,pl.ds(0,1024)],ld.at[i])
        z2=(z+order(i))%8
        for j in range(4):
            h=z2*4+(y+j)%4
            hot=hot_of(h)
            kv_out[h,0]=pick(k_vm,h,hot)
            kv_out[h,1]=pick(v_vm,h,hot)
    def pick_qg(i):
        z2=(z+order(i))%8
        for j in range(4):
            h=z2*4+(y+j)%4
            qg_out[h,0]=pick(q_vm,h,hot_of(h))
            qg_out[h,1]=g_vm[:,:,columns(h)]
    def to_plane(i, out, dst, send, recv):
        z2=(z+order(i))%8
        for j in range(4):
            y2=(y+j)%4
            src=out.at[z2*4+y2]
            if j:
                remote(src,dst,send,recv,device(x,z2,y2,c)).start()
            else:
                @pl.when(z2!=z)
                def _():
                    remote(src,dst,send,recv,device(x,z2,y2,c)).start()
                @pl.when(z2==z)
                def _():
                    pltpu.make_async_copy(src,dst,recv).start()
    def send_kv(i):
        to_plane(i,kv_out,kv.at[:,x_lo,z,x_hi,y,c],a_send.at[0],a_recv.at[i])
    def send_qg(i):
        to_plane(i,qg_out,qg_in.at[mine],b_send.at[0],b_recv.at[i])
    def ring(i):
        z2=(z+8-order(i))%8
        wait_for(kv_out.at[0:4],a_recv.at[i])
        own=chunk(x,z2)
        remote(own,own,x_send.at[0],x_recv.at[0,i],device(right,z,y,c)).start()
        remote(own,own,x_send.at[1],x_recv.at[1,i],device(left,z,y,c)).start()
        remote(own,own,c_send.at[0],c_recv.at[0],device(x,z,y,1-c)).start()
    def halves(i):
        z2=(z+8-order(i))%8
        for d,frm,to in ((0,left,right),(1,right,left)):
            a=chunk(frm,z2)
            wait_for(a,x_recv.at[d,i])
            ah=a.at[:,2*d:2*d+2]
            remote(ah,ah,f_send.at[d],f_recv.at[i],device(to,z,y,c)).start()
            remote(a,a,c_send.at[0],c_recv.at[0],device(x,z,y,1-c)).start()
    def last(i):
        z2=(z+8-order(i))%8
        a=chunk(far,z2)
        wait_for(a,f_recv.at[i])
        remote(a,a,c_send.at[0],c_recv.at[0],device(x,z,y,1-c)).start()
    def hand(s,first,count,unit,op):
        tile=unit//32; u=unit%32
        xo,co,t=owner(tile)
        src=qg_in.at[s,:,pl.ds(first,count)]; dst=qg.at[t,:,pl.ds(u,count)]
        @pl.when((xo!=x)|(co!=c))
        def _():
            cp=remote(src,dst,o_send.at[0],o_recv.at[0],device(xo,z,y,co))
            if op=="start": cp.start()
            else: cp.wait_send()
        if op=="start":
            @pl.when((xo==x)&(co==c))
            def _():
                pltpu.make_async_copy(src,dst,o_recv.at[0]).start()
    def spread(i,op):
        z2=(z+8-order(i))%8
        if op=="start":
            wait_for(qg_in.at[0:4],b_recv.at[i])
        def one(y2,_):
            s=z2*4+y2
            unit=(((x_lo*8+z2)*2+x_hi)*8+y2*2+c)*3
            @pl.when((unit%32)<=29)
            def _():
                hand(s,0,3,unit,op)
            @pl.when((unit%32)>29)
            def _():
                for e in range(3):
                    hand(s,e,1,unit+e,op)
            return 0
        lax.fori_loop(0,4,one,0)
    def loop(lo,hi,*acts):
        def body(i,_):
            for act in acts: act(i)
            return 0
        lax.fori_loop(lo,hi,body,0)
    def seq(lo,hi,*acts):
        loop(lo,hi,*[(lambda i,f=f,d=d: f(i+d)) for f,d in acts])
    def spread_start(i):
        spread(i,"start")
    fetch.wait()
    pick_kv(0)
    greeted()
    send_kv(0)
    loop(1,8,pick_kv,send_kv)
    wait_for(q_vm,ld.at[8]); wait_for(g_vm,ld.at[9])
    loop(0,8,pick_qg,send_qg)
    loop(0,4,ring)
    seq(4,8,(ring,0),(halves,-4))
    seq(4,8,(halves,0),(spread_start,-4))
    seq(0,4,(last,0),(spread_start,4))
    loop(4,8,last)
    wait_for(kv_out.at[0:31],a_send.at[0])
    wait_for(qg_out.at[0:31],b_send.at[0])
    loop(0,8,lambda i: spread(i,"done"))
    for d in range(2):
        wait_for(kv.at[:,0,:,0,:,0],x_send.at[d])
        wait_for(kv.at[:,0,:,0,0:2,0],f_send.at[d])
    wait_for(kv.at[:,:,:,:,:,0],c_send.at[0])
    wait_for(kv.at[:,:,:,:,:,0],c_recv.at[0])
    wait_for(qg,o_recv.at[0])

def gather(off,q,k,v,g):
    return pl.pallas_call(gather_kernel,
        out_shape=(pltpu.VMEM(KV,BF),pltpu.VMEM(QG,BF)),
        in_specs=[ANY]*5,
        out_specs=(VM,VM),
        scratch_shapes=[pltpu.VMEM((24,4,4096),BF)]*3+[pltpu.VMEM((3,8,4096),BF)]+[pltpu.VMEM((32,2,3,8,HD),BF)]*3+[
            pltpu.SMEM((HEADS,),jnp.int32),DMA((11,)),DMA((1,)),DMA((8,)),DMA((1,)),DMA((8,)),DMA((2,)),DMA((2,8)),DMA((2,)),DMA((8,)),DMA((1,)),DMA((1,)),DMA((1,)),DMA((1,))],
        name="gather",
        compiler_params=pltpu.CompilerParams(collective_id=0,has_side_effects=True,vmem_limit_bytes=40<<20))(*[afar(a) for a in (off,q,k,v,g)])

def scatter_kernel(dkv, og, out,
                   own, far_in, near_in, last_in, og_in, fin,
                   c_send, c_recv, g_send, g_recv, far_send, far_recv, near_send, last_send, fin_recv, p_send, p_recv):
    x_lo,z,x_hi,y,c=place()
    x=x_hi*2+x_lo
    right=(x+1)%4; left=(x+3)%4; far=(x+2)%4
    mine=z*4+y
    cols=pl.ds(pl.multiple_of(mine*HD,HD),HD)
    def at_z(i):
        return (z+order(7-i))%8
    greet(x,z,y,c)
    greeted()
    def back(op):
        def one(i,_):
            t=i//12; e=i%12
            blk=t*4+x+(t%2)*(3-2*x)
            tile=2*blk+(c+t)%2
            def hand(unit,count):
                piece=unit//3; k=unit%3; u=unit-tile*32
                xp=((piece//8)%2)*2+(piece//128)
                zp=(piece//16)%8; yp=(piece%8)//2; cp_=piece%2
                s=zp*4+yp
                src=og.at[t,:,pl.ds(u,count)]; dst=og_in.at[s,:,pl.ds(k,count)]
                sem=g_recv.at[zp]
                @pl.when((xp!=x)|(cp_!=c))
                def _():
                    cp=remote(src,dst,g_send.at[0],sem,device(xp,z,y,cp_))
                    if op=="start": cp.start()
                    else: cp.wait_send()
                if op=="start":
                    @pl.when((xp==x)&(cp_==c))
                    def _():
                        pltpu.make_async_copy(src,dst,sem).start()
            @pl.when(e<10)
            def _():
                hand(((tile*32+2)//3+e)*3,3)
            @pl.when(e>=10)
            def _():
                n=e-10; r=tile%3
                hand(tile*32+n+30*(1-(r+1)//2)+30*n*(r%2),1)
            return 0
        lax.fori_loop(0,36,one,0)
    for i in range(8):
        z2=at_z(i)
        remote(dkv.at[:,:,z2,:,:,1-c],own.at[:,:,z2],c_send.at[0],c_recv.at[i],device(x,z,y,1-c)).start()
    back("start")
    def to_rows(a, src, s, j):
        dst=out.at[2*a:2*a+2,:,:,cols]
        def away():
            remote(src,dst,p_send.at[a],p_recv.at[a],device(x,s//4,s%4,c)).start()
        if j:
            away()
        else:
            pl.when(s!=mine)(away)
            @pl.when(s==mine)
            def _():
                pltpu.make_async_copy(src,dst,p_recv.at[a]).start()
    def sum_cores(i):
        z2=at_z(i)
        wait_for(own.at[:,:,z2],c_recv.at[i])
        for xl in range(2):
            for xh in range(2):
                own[:,xl,z2,xh]=(own[:,xl,z2,xh].astype(F32)+dkv[:,xl,z2,xh,:,c].astype(F32)).astype(BF)
        ef=own.at[:,far%2,z2,far//2]
        remote(ef.at[:,0:2],far_in.at[0,z2],far_send.at[0],far_recv.at[0,i],device(right,z,y,c)).start()
        remote(ef.at[:,2:4],far_in.at[1,z2],far_send.at[0],far_recv.at[1,i],device(left,z,y,c)).start()
    def rows_back(i):
        z2=at_z(i)
        wait_for(og_in.at[0:4],g_recv.at[z2])
        for j in range(4):
            s=z2*4+(y+j)%4
            to_rows(0,og_in.at[s],s,j)
    def relay(i):
        z2=at_z(i)
        for d,peer in ((0,right),(1,left)):
            lo=2*d
            buf=far_in.at[d,z2]
            wait_for(buf,far_recv.at[d,i])
            far_in[d,z2]=(far_in[d,z2].astype(F32)+own[:,peer%2,z2,peer//2,lo:lo+2].astype(F32)).astype(BF)
            remote(buf,last_in.at[d,z2],last_send.at[0],fin_recv.at[i],device(peer,z,y,c)).start()
        er=own.at[:,right%2,z2,right//2]; el=own.at[:,left%2,z2,left//2]
        remote(er.at[:,2:4],near_in.at[0,z2],near_send.at[0],fin_recv.at[i],device(right,z,y,c)).start()
        remote(el.at[:,0:2],near_in.at[1,z2],near_send.at[0],fin_recv.at[i],device(left,z,y,c)).start()
    def finish(i):
        z2=at_z(i)
        wait_for(own.at[:,0,z2],fin_recv.at[i])
        for d in range(2):
            lo=2*d
            fin[:,pl.ds(z2*4+lo,2)]=(own[:,x_lo,z2,x_hi,lo:lo+2].astype(F32)+last_in[d,z2].astype(F32)+near_in[1-d,z2].astype(F32)).astype(BF)
        for j in range(4):
            s=z2*4+(y+j)%4
            to_rows(1,fin.at[:,s],s,j)
    def loop(lo,hi,*acts):
        def body(i,_):
            for act in acts: act(i)
            return 0
        lax.fori_loop(lo,hi,body,0)
    loop(0,8,sum_cores)
    loop(0,8,rows_back)
    loop(0,4,relay)
    loop(4,8,relay,lambda i: finish(i-4))
    loop(4,8,finish)
    back("done")
    wait_for(own,c_send.at[0])
    for b,sem in ((far_in,far_send),(near_in,near_send),(last_in,last_send)):
        wait_for(b,sem.at[0])
    wait_for(og_in.at[0:31],p_send.at[0])
    wait_for(fin.at[:,0:31],p_send.at[1])
    for a in range(2):
        wait_for(out.at[2*a:2*a+2],p_recv.at[a])

def scatter(dkv,og):
    return pl.pallas_call(scatter_kernel,
        out_shape=pltpu.VMEM((4,3,8,4096),BF),
        in_specs=[VM]*2,
        out_specs=VM,
        scratch_shapes=[pltpu.VMEM((2,2,8,2,4,3,8,HD),BF)]+[pltpu.VMEM((2,8,2,2,3,8,HD),BF)]*3+[pltpu.VMEM((32,2,3,8,HD),BF),pltpu.VMEM((2,32,3,8,HD),BF),
            DMA((1,)),DMA((8,)),DMA((1,)),DMA((8,)),DMA((1,)),DMA((2,8)),DMA((1,)),DMA((1,)),DMA((8,)),DMA((2,)),DMA((2,))],
        name="scatter",
        compiler_params=pltpu.CompilerParams(collective_id=1,has_side_effects=True,vmem_limit_bytes=40<<20))(held(dkv),held(og))

def settle_kernel(src,*refs):
    cps=[pltpu.make_async_copy(src.at[i],refs[i],refs[4].at[i]) for i in range(4)]
    for cp in cps: cp.start()
    for cp in cps: cp.wait()

def settle(out):
    return pl.pallas_call(settle_kernel,
        out_shape=(jax.ShapeDtypeStruct((3,8,4096),BF),)*4,
        in_specs=[VM],out_specs=(ANY,)*4,
        scratch_shapes=[DMA((4,))],
        name="settle",
        compiler_params=pltpu.CompilerParams(vmem_limit_bytes=40<<20))(held(out))

def on_device(queries,key_states,value_states,out_grad,offsets,block_mask):
    kv,qg=gather(offsets,queries,key_states,value_states,out_grad.reshape(3,8,4096))
    dkv,og=attend(block_mask,kv,qg)
    outs=settle(scatter(dkv,og))
    return tuple(o.reshape(24,4096) for o in outs)


def solution(mesh):
    rows3=P(("ctx","head"),None,None); rows2=P(("ctx","head"),None)
    return jax.shard_map(on_device,mesh=mesh,in_specs=(rows3,rows3,rows3,rows2,P(),P()),
                         out_specs=(rows2,)*4,check_vma=False)
```

```python
import functools, jax, jax.numpy as jnp
from jax.sharding import PartitionSpec as P
from jax import lax
from jax.experimental import pallas as pl
from jax.experimental.pallas import tpu as pltpu
BF=jnp.bfloat16; F32=jnp.float32
HEADS=32; NB=12; BLK=512; TQ=256; HD=128
SCALE=HD**-0.5
C2=SCALE*1.4426950408889634
FU=4; GB=4

def dot(a,b):
    return jnp.dot(a,b,preferred_element_type=F32)

def dot_t(a,b):
    return lax.dot_general(a,b,(((0,),(0,)),((),())),preferred_element_type=F32)

def entry(table,k):
    return table//((1+3*(k%2))*(1+15*(k//2)))%4

def block_of(x,t):
    return t*4+entry(228+(75-228)*(t%2)+(54-228)*(t//2),x)

def chip_of(blk):
    t=blk//4
    return entry(228+(30-228)*(t%2)+(135-228)*(t//2),blk%4)

def my_tiles():
    ctx=lax.axis_index("ctx"); hd=lax.axis_index("head")
    return (hd//8)*2+ctx//8, hd%2

def attend_kernel(mask_hbm, kv_ref, qg_ref, dkv_ref, og_ref,
                  p_sc, m_sc, dk_acc, dv_acc, ot_acc, dqt_acc, s_sc, qt_sc, gt_sc, st_sc, live, pair_tile, mask_ref, ld):
    grp,core=my_tiles()
    fetch=pltpu.make_async_copy(mask_hbm,mask_ref,ld.at[0])
    fetch.start()
    kv_rows=kv_ref.reshape(2,768,8,HD)
    dkv_rows=dkv_ref.reshape(2,768,8,HD)
    def blk(i,j):
        return kv_rows[i,pl.ds(pl.multiple_of(j*64,64),64)].reshape(BLK,HD)
    @pl.loop(0,NB)
    def _(j):
        z=jnp.zeros((BLK,HD),F32)
        rows=pl.ds(pl.multiple_of(j*BLK,BLK),BLK)
        dk_acc[rows]=z; dv_acc[rows]=z
    def groups(first,n_live,step,size,c):
        start=first
        while size:
            count=(n_live-start)//size
            def run(i,c,start=start,size=size):
                return step(start+i*size,size,c)
            c=lax.fori_loop(0,count,run,c)
            start=start+count*size
            size//=2
        return c
    def tile_of(t):
        return block_of(grp,t), (core+t)%2
    def note(n,t,j):
        live[n]=j
        pair_tile[n]=t
    def list_blocks(t,n):
        def one(j,n):
            note(n,t,j)
            return n+mask_ref[tile_of(t)[0],j]
        return lax.fori_loop(0,tile_of(t)[0],one,n)
    def exps(t,slot,s,m_old,m):
        mc=m*C2
        alpha=jnp.exp2(m_old*C2-mc)
        p=jnp.exp2(s*C2-mc)
        pb=p.astype(BF)
        p_sc[slot]=pb
        m_sc[slot]=m
        return alpha,jnp.sum(p,axis=0,keepdims=True),pb
    def diagonals():
        for t in range(3):
            qt_sc[t]=qg_ref[t,0].reshape(TQ,HD).T
            gt_sc[t]=qg_ref[t,1].reshape(TQ,HD).T
        for t in range(3):
            b,half=tile_of(t)
            s=dot(blk(0,b),qt_sc[t])
            kr=lax.broadcasted_iota(jnp.int32,(BLK,TQ),0); qc=lax.broadcasted_iota(jnp.int32,(BLK,TQ),1)+half*TQ
            s=jnp.where(kr<=qc,s,-1e30)
            m=jnp.max(s,axis=0,keepdims=True)
            _,l,pb=exps(t,t,s,m,m)
            st_sc[t,0]=m; st_sc[t,1]=l; st_sc[t,2]=m
            ot_acc[t]=dot_t(blk(1,b),pb)
    def ahead(i,slot):
        t=pair_tile[i]
        s=dot(blk(0,live[i]),qt_sc[t])
        s_sc[slot]=s
        m=jnp.maximum(st_sc[t,2],jnp.max(s,axis=0,keepdims=True))
        st_sc[t,2]=m
        return m
    def fwd(i,cur,m):
        m_next=ahead(i+1,1-cur)
        t=pair_tile[i]
        alpha,total,pb=exps(t,i,s_sc[cur],st_sc[t,0],m)
        st_sc[t,0]=m
        st_sc[t,1]=st_sc[t,1]*alpha+total
        ot_acc[t]=ot_acc[t]*alpha+dot_t(blk(1,live[i]),pb)
        return m_next
    def fwds(i,size,m):
        for e in range(size): m=fwd(i+e,(e+1)%2,m)
        return m
    def finish():
        for t in range(3):
            inv=1.0/st_sc[t,1]
            ot=(ot_acc[t]*inv).astype(BF)
            og_ref[t,0]=ot.T.reshape(32,8,HD)
            st_sc[t,0]=st_sc[t,0]*C2
            st_sc[t,1]=inv
            st_sc[t,2]=jnp.sum(gt_sc[t].astype(F32)*ot.astype(F32),axis=0,keepdims=True)
            dqt_acc[t]=jnp.zeros((HD,TQ),F32)
    def bwd(i,size,c):
        for e in range(size):
            slot=i+e; j=live[slot]; t=pair_tile[slot]
            gt=gt_sc[t]; q=qg_ref[t,0].reshape(TQ,HD); g=qg_ref[t,1].reshape(TQ,HD)
            f=jnp.exp2(m_sc[slot]*C2-st_sc[t,0])*st_sc[t,1]
            p=p_sc[slot].astype(F32)*f
            dp=dot(blk(1,j),gt)
            ds=(p*(dp-st_sc[t,2])).astype(BF)
            rows=pl.ds(pl.multiple_of(j*BLK,BLK),BLK)
            dv_acc[rows]+=dot(p.astype(BF),g)
            dk_acc[rows]+=dot(ds,q)
            dqt_acc[t]+=dot_t(blk(0,j),ds)
        return c
    def settle_blocks(lo,hi):
        @pl.loop(lo,hi)
        def _(j):
            rows=pl.ds(pl.multiple_of(j*BLK,BLK),BLK)
            un=pl.ds(pl.multiple_of(j*64,64),64)
            dkv_rows[0,un]=(dk_acc[rows]*SCALE).astype(BF).reshape(64,8,HD)
            dkv_rows[1,un]=dv_acc[rows].astype(BF).reshape(64,8,HD)
    diagonals()
    fetch.wait()
    for t in range(3): note(t,t,tile_of(t)[0])
    pairs=3
    for t in range(3): pairs=list_blocks(t,pairs)
    note(pairs,0,0)
    groups(3,pairs,fwds,FU,ahead(3,1))
    finish()
    groups(0,pairs,bwd,GB,0)
    for t in range(3):
        og_ref[t,1]=(dqt_acc[t]*SCALE).astype(BF).T.reshape(32,8,HD)
    settle_blocks(0,NB)

KV=(2,2,8,2,4,2,3,8,HD)
QG=(3,2,32,8,HD)
VM=pl.BlockSpec(memory_space=pltpu.VMEM)
ANY=pl.BlockSpec(memory_space=pl.ANY)
DMA=pltpu.SemaphoreType.DMA
def held(x):
    return pltpu.with_memory_space_constraint(x,pltpu.VMEM)
def afar(x):
    return pltpu.with_memory_space_constraint(x,pltpu.HBM)
def attend(mask,kv,qg):
    return pl.pallas_call(attend_kernel,
        out_shape=(pltpu.VMEM(KV,BF),pltpu.VMEM(QG,BF)),
        in_specs=[ANY,VM,VM],
        out_specs=(VM,VM),
        scratch_shapes=[
            pltpu.VMEM((3*NB,BLK,TQ),BF),pltpu.VMEM((3*NB,1,TQ),F32),pltpu.VMEM((NB*BLK,HD),F32),pltpu.VMEM((NB*BLK,HD),F32),
            pltpu.VMEM((3,HD,TQ),F32),pltpu.VMEM((3,HD,TQ),F32),pltpu.VMEM((2,BLK,TQ),F32),pltpu.VMEM((3,HD,TQ),BF),pltpu.VMEM((3,HD,TQ),BF),pltpu.VMEM((3,3,1,TQ),F32),pltpu.SMEM((3*NB+1,),jnp.int32),pltpu.SMEM((3*NB+1,),jnp.int32),pltpu.SMEM((NB,NB),jnp.int32),DMA((1,))],
        name="attend",
        compiler_params=pltpu.CompilerParams(vmem_limit_bytes=40<<20))(afar(mask),held(kv),held(qg))

MESH=pl.DeviceIdType.MESH

def place():
    ctx=lax.axis_index("ctx"); hd=lax.axis_index("head")
    return ctx//8, ctx%8, hd//8, (hd%8)//2, hd%2

def device(x, z, y, c):
    return ((x%2)*8+z, (x//2)*8+y*2+c)

def owner(tile):
    blk=tile//2; t=blk//4
    return chip_of(blk), (tile%2+t)%2, t

def order(i):
    return (i%2)*((i+1)//2)+(1-i%2)*((8-i//2)%8)

def remote(src, dst, send, recv, dev):
    return pltpu.make_async_remote_copy(src_ref=src, dst_ref=dst, send_sem=send, recv_sem=recv,
                                        device_id=dev, device_id_type=MESH)

def wait_for(ref, sem):
    pltpu.make_async_copy(ref,ref,sem).wait()

def greet(x, z, y, c):
    barrier=pltpu.get_barrier_semaphore()
    def plane(i,_):
        s=(z*4+y+i)%32
        pl.semaphore_signal(barrier, inc=1, device_id=device(x,s//4,s%4,c), device_id_type=MESH)
        return 0
    lax.fori_loop(1,32,plane,0,unroll=True)
    for i in range(1,8):
        s=(x*2+c+i)%8
        pl.semaphore_signal(barrier, inc=1, device_id=device(s//2,z,y,s%2), device_id_type=MESH)

def greeted():
    pl.semaphore_wait(pltpu.get_barrier_semaphore(), 38)

def gather_kernel(off_hbm, q, k, v, g, kv, qg, q_vm, k_vm, v_vm, g_vm, kv_out, qg_out, qg_in,
                  off, ld, a_send, a_recv, b_send, b_recv, x_send, x_recv, f_send, f_recv, c_send, c_recv, o_send, o_recv):
    x_lo,z,x_hi,y,c=place()
    x=x_hi*2+x_lo
    right=(x+1)%4; left=(x+3)%4; far=(x+2)%4
    mine=z*4+y
    greet(x,z,y,c)
    for i in range(8):
        cols=pl.ds(pl.multiple_of(((z+order(i))%8)*512,512),512)
        pltpu.make_async_copy(k.at[:,:,cols],k_vm.at[:,:,cols],ld.at[i]).start()
        pltpu.make_async_copy(v.at[:,:,cols],v_vm.at[:,:,cols],ld.at[i]).start()
    pltpu.make_async_copy(q,q_vm,ld.at[8]).start()
    pltpu.make_async_copy(g,g_vm,ld.at[9]).start()
    fetch=pltpu.make_async_copy(off_hbm,off,ld.at[10])
    fetch.start()
    row=lax.broadcasted_iota(jnp.int32,(24,96),0); col=lax.broadcasted_iota(jnp.int32,(24,96),1)
    lead=col-row*4
    def columns(h):
        return pl.ds(pl.multiple_of(h*HD,HD),HD)
    def pick(ref,h,hot):
        return dot(hot,ref[:,:,columns(h)].reshape(96,HD)).reshape(3,8,HD).astype(BF)
    def hot_of(h):
        return (lead==off[h]).astype(F32).astype(BF)
    def chunk(x2,z2):
        return kv.at[:,x2%2,z2,x2//2,:,c]
    def pick_kv(i):
        wait_for(k_vm.at[:,:,pl.ds(0,1024)],ld.at[i])
        z2=(z+order(i))%8
        for j in range(4):
            h=z2*4+(y+j)%4
            hot=hot_of(h)
            kv_out[h,0]=pick(k_vm,h,hot)
            kv_out[h,1]=pick(v_vm,h,hot)
    def pick_qg(i):
        z2=(z+order(i))%8
        for j in range(4):
            h=z2*4+(y+j)%4
            qg_out[h,0]=pick(q_vm,h,hot_of(h))
            qg_out[h,1]=g_vm[:,:,columns(h)]
    def to_plane(i, out, dst, send, recv):
        z2=(z+order(i))%8
        for j in range(4):
            y2=(y+j)%4
            src=out.at[z2*4+y2]
            if j:
                remote(src,dst,send,recv,device(x,z2,y2,c)).start()
            else:
                @pl.when(z2!=z)
                def _():
                    remote(src,dst,send,recv,device(x,z2,y2,c)).start()
                @pl.when(z2==z)
                def _():
                    pltpu.make_async_copy(src,dst,recv).start()
    def send_kv(i):
        to_plane(i,kv_out,kv.at[:,x_lo,z,x_hi,y,c],a_send.at[0],a_recv.at[i])
    def send_qg(i):
        to_plane(i,qg_out,qg_in.at[mine],b_send.at[0],b_recv.at[i])
    def ring(i):
        z2=(z+8-order(i))%8
        wait_for(kv_out.at[0:4],a_recv.at[i])
        own=chunk(x,z2)
        remote(own,own,x_send.at[0],x_recv.at[0,i],device(right,z,y,c)).start()
        remote(own,own,x_send.at[1],x_recv.at[1,i],device(left,z,y,c)).start()
        remote(own,own,c_send.at[0],c_recv.at[0],device(x,z,y,1-c)).start()
    def halves(i):
        z2=(z+8-order(i))%8
        for d,frm,to in ((0,left,right),(1,right,left)):
            a=chunk(frm,z2)
            wait_for(a,x_recv.at[d,i])
            ah=a.at[:,2*d:2*d+2]
            remote(ah,ah,f_send.at[d],f_recv.at[i],device(to,z,y,c)).start()
            remote(a,a,c_send.at[0],c_recv.at[0],device(x,z,y,1-c)).start()
    def last(i):
        z2=(z+8-order(i))%8
        a=chunk(far,z2)
        wait_for(a,f_recv.at[i])
        remote(a,a,c_send.at[0],c_recv.at[0],device(x,z,y,1-c)).start()
    def hand(s,first,count,unit,op):
        tile=unit//32; u=unit%32
        xo,co,t=owner(tile)
        src=qg_in.at[s,:,pl.ds(first,count)]; dst=qg.at[t,:,pl.ds(u,count)]
        @pl.when((xo!=x)|(co!=c))
        def _():
            cp=remote(src,dst,o_send.at[0],o_recv.at[0],device(xo,z,y,co))
            if op=="start": cp.start()
            else: cp.wait_send()
        if op=="start":
            @pl.when((xo==x)&(co==c))
            def _():
                pltpu.make_async_copy(src,dst,o_recv.at[0]).start()
    def spread(i,op):
        z2=(z+8-order(i))%8
        if op=="start":
            wait_for(qg_in.at[0:4],b_recv.at[i])
        def one(y2,_):
            s=z2*4+y2
            unit=(((x_lo*8+z2)*2+x_hi)*8+y2*2+c)*3
            @pl.when((unit%32)<=29)
            def _():
                hand(s,0,3,unit,op)
            @pl.when((unit%32)>29)
            def _():
                for e in range(3):
                    hand(s,e,1,unit+e,op)
            return 0
        lax.fori_loop(0,4,one,0)
    def loop(lo,hi,*acts):
        def body(i,_):
            for act in acts: act(i)
            return 0
        lax.fori_loop(lo,hi,body,0)
    def seq(lo,hi,*acts):
        loop(lo,hi,*[(lambda i,f=f,d=d: f(i+d)) for f,d in acts])
    def spread_start(i):
        spread(i,"start")
    fetch.wait()
    pick_kv(0)
    greeted()
    send_kv(0)
    loop(1,8,pick_kv,send_kv)
    wait_for(q_vm,ld.at[8]); wait_for(g_vm,ld.at[9])
    loop(0,8,pick_qg,send_qg)
    loop(0,4,ring)
    seq(4,8,(ring,0),(halves,-4))
    seq(4,8,(halves,0),(spread_start,-4))
    seq(0,4,(last,0),(spread_start,4))
    loop(4,8,last)
    wait_for(kv_out.at[0:31],a_send.at[0])
    wait_for(qg_out.at[0:31],b_send.at[0])
    loop(0,8,lambda i: spread(i,"done"))
    for d in range(2):
        wait_for(kv.at[:,0,:,0,:,0],x_send.at[d])
        wait_for(kv.at[:,0,:,0,0:2,0],f_send.at[d])
    wait_for(kv.at[:,:,:,:,:,0],c_send.at[0])
    wait_for(kv.at[:,:,:,:,:,0],c_recv.at[0])
    wait_for(qg,o_recv.at[0])

def gather(off,q,k,v,g):
    return pl.pallas_call(gather_kernel,
        out_shape=(pltpu.VMEM(KV,BF),pltpu.VMEM(QG,BF)),
        in_specs=[ANY]*5,
        out_specs=(VM,VM),
        scratch_shapes=[pltpu.VMEM((24,4,4096),BF)]*3+[pltpu.VMEM((3,8,4096),BF)]+[pltpu.VMEM((32,2,3,8,HD),BF)]*3+[
            pltpu.SMEM((HEADS,),jnp.int32),DMA((11,)),DMA((1,)),DMA((8,)),DMA((1,)),DMA((8,)),DMA((2,)),DMA((2,8)),DMA((2,)),DMA((8,)),DMA((1,)),DMA((1,)),DMA((1,)),DMA((1,))],
        name="gather",
        compiler_params=pltpu.CompilerParams(collective_id=0,has_side_effects=True,vmem_limit_bytes=40<<20))(*[afar(a) for a in (off,q,k,v,g)])

def scatter_kernel(dkv, og, out,
                   own, far_in, near_in, last_in, og_in, fin,
                   c_send, c_recv, g_send, g_recv, far_send, far_recv, near_send, last_send, fin_recv, p_send, p_recv):
    x_lo,z,x_hi,y,c=place()
    x=x_hi*2+x_lo
    right=(x+1)%4; left=(x+3)%4; far=(x+2)%4
    mine=z*4+y
    cols=pl.ds(pl.multiple_of(mine*HD,HD),HD)
    def at_z(i):
        return (z+order(7-i))%8
    greet(x,z,y,c)
    greeted()
    def back(op):
        def one(i,_):
            t=i//12; e=i%12
            blk=block_of(x,t)
            tile=2*blk+(c+t)%2
            def hand(unit,count):
                piece=unit//3; k=unit%3; u=unit-tile*32
                xp=((piece//8)%2)*2+(piece//128)
                zp=(piece//16)%8; yp=(piece%8)//2; cp_=piece%2
                s=zp*4+yp
                src=og.at[t,:,pl.ds(u,count)]; dst=og_in.at[s,:,pl.ds(k,count)]
                sem=g_recv.at[zp]
                @pl.when((xp!=x)|(cp_!=c))
                def _():
                    cp=remote(src,dst,g_send.at[0],sem,device(xp,z,y,cp_))
                    if op=="start": cp.start()
                    else: cp.wait_send()
                if op=="start":
                    @pl.when((xp==x)&(cp_==c))
                    def _():
                        pltpu.make_async_copy(src,dst,sem).start()
            @pl.when(e<10)
            def _():
                hand(((tile*32+2)//3+e)*3,3)
            @pl.when(e>=10)
            def _():
                n=e-10; r=tile%3
                hand(tile*32+n+30*(1-(r+1)//2)+30*n*(r%2),1)
            return 0
        lax.fori_loop(0,36,one,0)
    for i in range(8):
        z2=at_z(i)
        remote(dkv.at[:,:,z2,:,:,1-c],own.at[:,:,z2],c_send.at[0],c_recv.at[i],device(x,z,y,1-c)).start()
    back("start")
    def to_rows(a, src, s, j):
        dst=out.at[2*a:2*a+2,:,:,cols]
        def away():
            remote(src,dst,p_send.at[a],p_recv.at[a],device(x,s//4,s%4,c)).start()
        if j:
            away()
        else:
            pl.when(s!=mine)(away)
            @pl.when(s==mine)
            def _():
                pltpu.make_async_copy(src,dst,p_recv.at[a]).start()
    def sum_cores(i):
        z2=at_z(i)
        wait_for(own.at[:,:,z2],c_recv.at[i])
        for xl in range(2):
            for xh in range(2):
                own[:,xl,z2,xh]=(own[:,xl,z2,xh].astype(F32)+dkv[:,xl,z2,xh,:,c].astype(F32)).astype(BF)
        ef=own.at[:,far%2,z2,far//2]
        remote(ef.at[:,0:2],far_in.at[0,z2],far_send.at[0],far_recv.at[0,i],device(right,z,y,c)).start()
        remote(ef.at[:,2:4],far_in.at[1,z2],far_send.at[0],far_recv.at[1,i],device(left,z,y,c)).start()
    def rows_back(i):
        z2=at_z(i)
        wait_for(og_in.at[0:4],g_recv.at[z2])
        for j in range(4):
            s=z2*4+(y+j)%4
            to_rows(0,og_in.at[s],s,j)
    def relay(i):
        z2=at_z(i)
        for d,peer in ((0,right),(1,left)):
            lo=2*d
            buf=far_in.at[d,z2]
            wait_for(buf,far_recv.at[d,i])
            far_in[d,z2]=(far_in[d,z2].astype(F32)+own[:,peer%2,z2,peer//2,lo:lo+2].astype(F32)).astype(BF)
            remote(buf,last_in.at[d,z2],last_send.at[0],fin_recv.at[i],device(peer,z,y,c)).start()
        er=own.at[:,right%2,z2,right//2]; el=own.at[:,left%2,z2,left//2]
        remote(er.at[:,2:4],near_in.at[0,z2],near_send.at[0],fin_recv.at[i],device(right,z,y,c)).start()
        remote(el.at[:,0:2],near_in.at[1,z2],near_send.at[0],fin_recv.at[i],device(left,z,y,c)).start()
    def finish(i):
        z2=at_z(i)
        wait_for(own.at[:,0,z2],fin_recv.at[i])
        for d in range(2):
            lo=2*d
            fin[:,pl.ds(z2*4+lo,2)]=(own[:,x_lo,z2,x_hi,lo:lo+2].astype(F32)+last_in[d,z2].astype(F32)+near_in[1-d,z2].astype(F32)).astype(BF)
        for j in range(4):
            s=z2*4+(y+j)%4
            to_rows(1,fin.at[:,s],s,j)
    def loop(lo,hi,*acts):
        def body(i,_):
            for act in acts: act(i)
            return 0
        lax.fori_loop(lo,hi,body,0)
    loop(0,8,sum_cores)
    loop(0,8,rows_back)
    loop(0,4,relay)
    loop(4,8,relay,lambda i: finish(i-4))
    loop(4,8,finish)
    back("done")
    wait_for(own,c_send.at[0])
    for b,sem in ((far_in,far_send),(near_in,near_send),(last_in,last_send)):
        wait_for(b,sem.at[0])
    wait_for(og_in.at[0:31],p_send.at[0])
    wait_for(fin.at[:,0:31],p_send.at[1])
    for a in range(2):
        wait_for(out.at[2*a:2*a+2],p_recv.at[a])

def scatter(dkv,og):
    return pl.pallas_call(scatter_kernel,
        out_shape=pltpu.VMEM((4,3,8,4096),BF),
        in_specs=[VM]*2,
        out_specs=VM,
        scratch_shapes=[pltpu.VMEM((2,2,8,2,4,3,8,HD),BF)]+[pltpu.VMEM((2,8,2,2,3,8,HD),BF)]*3+[pltpu.VMEM((32,2,3,8,HD),BF),pltpu.VMEM((2,32,3,8,HD),BF),
            DMA((1,)),DMA((8,)),DMA((1,)),DMA((8,)),DMA((1,)),DMA((2,8)),DMA((1,)),DMA((1,)),DMA((8,)),DMA((2,)),DMA((2,))],
        name="scatter",
        compiler_params=pltpu.CompilerParams(collective_id=1,has_side_effects=True,vmem_limit_bytes=40<<20))(held(dkv),held(og))

def settle_kernel(src,*refs):
    cps=[pltpu.make_async_copy(src.at[i],refs[i],refs[4].at[i]) for i in range(4)]
    for cp in cps: cp.start()
    for cp in cps: cp.wait()

def settle(out):
    return pl.pallas_call(settle_kernel,
        out_shape=(jax.ShapeDtypeStruct((3,8,4096),BF),)*4,
        in_specs=[VM],out_specs=(ANY,)*4,
        scratch_shapes=[DMA((4,))],
        name="settle",
        compiler_params=pltpu.CompilerParams(vmem_limit_bytes=40<<20))(held(out))

def on_device(queries,key_states,value_states,out_grad,offsets,block_mask):
    kv,qg=gather(offsets,queries,key_states,value_states,out_grad.reshape(3,8,4096))
    dkv,og=attend(block_mask,kv,qg)
    outs=settle(scatter(dkv,og))
    return tuple(o.reshape(24,4096) for o in outs)


def solution(mesh):
    rows3=P(("ctx","head"),None,None); rows2=P(("ctx","head"),None)
    return jax.shard_map(on_device,mesh=mesh,in_specs=(rows3,rows3,rows3,rows2,P(),P()),
                         out_specs=(rows2,)*4,check_vma=False)
```

```python
import functools, jax, jax.numpy as jnp
from jax.sharding import PartitionSpec as P
from jax import lax
from jax.experimental import pallas as pl
from jax.experimental.pallas import tpu as pltpu
BF=jnp.bfloat16; F32=jnp.float32
HEADS=32; NB=12; BLK=512; TQ=256; HD=128
SCALE=HD**-0.5
C2=SCALE*1.4426950408889634
FU=4; GB=8

def dot(a,b):
    return jnp.dot(a,b,preferred_element_type=F32)

def dot_t(a,b):
    return lax.dot_general(a,b,(((0,),(0,)),((),())),preferred_element_type=F32)

def entry(table,k):
    return table//((1+3*(k%2))*(1+15*(k//2)))%4

def block_of(x,t):
    return t*4+entry(228+(75-228)*(t%2)+(54-228)*(t//2),x)

def chip_of(blk):
    t=blk//4
    return entry(228+(30-228)*(t%2)+(135-228)*(t//2),blk%4)

def my_tiles():
    ctx=lax.axis_index("ctx"); hd=lax.axis_index("head")
    return (hd//8)*2+ctx//8, hd%2

def attend_kernel(mask_hbm, kv_ref, qg_ref, dkv_ref, og_ref,
                  p_sc, m_sc, dk_acc, dv_acc, ot_acc, dqt_acc, s_sc, qt_sc, gt_sc, st_sc, live, pair_tile, mask_ref, ld):
    grp,core=my_tiles()
    fetch=pltpu.make_async_copy(mask_hbm,mask_ref,ld.at[0])
    fetch.start()
    kv_rows=kv_ref.reshape(2,768,8,HD)
    dkv_rows=dkv_ref.reshape(2,768,8,HD)
    def blk(i,j):
        return kv_rows[i,pl.ds(pl.multiple_of(j*64,64),64)].reshape(BLK,HD)
    @pl.loop(0,NB)
    def _(j):
        z=jnp.zeros((BLK,HD),F32)
        rows=pl.ds(pl.multiple_of(j*BLK,BLK),BLK)
        dk_acc[rows]=z; dv_acc[rows]=z
    def groups(first,n_live,step,size,c):
        start=first
        while size:
            count=(n_live-start)//size
            def run(i,c,start=start,size=size):
                return step(start+i*size,size,c)
            c=lax.fori_loop(0,count,run,c)
            start=start+count*size
            size//=2
        return c
    def tile_of(t):
        return block_of(grp,t), (core+t)%2
    def note(n,t,j):
        live[n]=j
        pair_tile[n]=t
    def list_blocks(t,n):
        def one(j,n):
            note(n,t,j)
            return n+mask_ref[tile_of(t)[0],j]
        return lax.fori_loop(0,tile_of(t)[0],one,n)
    def exps(t,slot,s,m_old,m):
        mc=m*C2
        alpha=jnp.exp2(m_old*C2-mc)
        p=jnp.exp2(s*C2-mc)
        pb=p.astype(BF)
        p_sc[slot]=pb
        m_sc[slot]=m
        return alpha,jnp.sum(p,axis=0,keepdims=True),pb
    def diagonals():
        for t in range(3):
            qt_sc[t]=qg_ref[t,0].reshape(TQ,HD).T
            gt_sc[t]=qg_ref[t,1].reshape(TQ,HD).T
        for t in range(3):
            b,half=tile_of(t)
            s=dot(blk(0,b),qt_sc[t])
            kr=lax.broadcasted_iota(jnp.int32,(BLK,TQ),0); qc=lax.broadcasted_iota(jnp.int32,(BLK,TQ),1)+half*TQ
            s=jnp.where(kr<=qc,s,-1e30)
            m=jnp.max(s,axis=0,keepdims=True)
            _,l,pb=exps(t,t,s,m,m)
            st_sc[t,0]=m; st_sc[t,1]=l; st_sc[t,2]=m
            ot_acc[t]=dot_t(blk(1,b),pb)
    def ahead(i,slot):
        t=pair_tile[i]
        s=dot(blk(0,live[i]),qt_sc[t])
        s_sc[slot]=s
        m=jnp.maximum(st_sc[t,2],jnp.max(s,axis=0,keepdims=True))
        st_sc[t,2]=m
        return m
    def fwd(i,cur,m):
        m_next=ahead(i+1,1-cur)
        t=pair_tile[i]
        alpha,total,pb=exps(t,i,s_sc[cur],st_sc[t,0],m)
        st_sc[t,0]=m
        st_sc[t,1]=st_sc[t,1]*alpha+total
        ot_acc[t]=ot_acc[t]*alpha+dot_t(blk(1,live[i]),pb)
        return m_next
    def fwds(i,size,m):
        for e in range(size): m=fwd(i+e,(e+1)%2,m)
        return m
    def finish():
        for t in range(3):
            inv=1.0/st_sc[t,1]
            ot=(ot_acc[t]*inv).astype(BF)
            og_ref[t,0]=ot.T.reshape(32,8,HD)
            st_sc[t,0]=st_sc[t,0]*C2
            st_sc[t,1]=inv
            st_sc[t,2]=jnp.sum(gt_sc[t].astype(F32)*ot.astype(F32),axis=0,keepdims=True)
            dqt_acc[t]=jnp.zeros((HD,TQ),F32)
    def bwd(i,size,c):
        for e in range(size):
            slot=i+e; j=live[slot]; t=pair_tile[slot]
            gt=gt_sc[t]; q=qg_ref[t,0].reshape(TQ,HD); g=qg_ref[t,1].reshape(TQ,HD)
            f=jnp.exp2(m_sc[slot]*C2-st_sc[t,0])*st_sc[t,1]
            p=p_sc[slot].astype(F32)*f
            dp=dot(blk(1,j),gt)
            ds=(p*(dp-st_sc[t,2])).astype(BF)
            rows=pl.ds(pl.multiple_of(j*BLK,BLK),BLK)
            dv_acc[rows]+=dot(p.astype(BF),g)
            dk_acc[rows]+=dot(ds,q)
            dqt_acc[t]+=dot_t(blk(0,j),ds)
        return c
    def settle_blocks(lo,hi):
        @pl.loop(lo,hi)
        def _(j):
            rows=pl.ds(pl.multiple_of(j*BLK,BLK),BLK)
            un=pl.ds(pl.multiple_of(j*64,64),64)
            dkv_rows[0,un]=(dk_acc[rows]*SCALE).astype(BF).reshape(64,8,HD)
            dkv_rows[1,un]=dv_acc[rows].astype(BF).reshape(64,8,HD)
    diagonals()
    fetch.wait()
    for t in range(3): note(t,t,tile_of(t)[0])
    pairs=3
    for t in range(3): pairs=list_blocks(t,pairs)
    note(pairs,0,0)
    groups(3,pairs,fwds,FU,ahead(3,1))
    finish()
    groups(0,pairs,bwd,GB,0)
    for t in range(3):
        og_ref[t,1]=(dqt_acc[t]*SCALE).astype(BF).T.reshape(32,8,HD)
    settle_blocks(0,NB)

KV=(2,2,8,2,4,2,3,8,HD)
QG=(3,2,32,8,HD)
VM=pl.BlockSpec(memory_space=pltpu.VMEM)
ANY=pl.BlockSpec(memory_space=pl.ANY)
DMA=pltpu.SemaphoreType.DMA
def held(x):
    return pltpu.with_memory_space_constraint(x,pltpu.VMEM)
def afar(x):
    return pltpu.with_memory_space_constraint(x,pltpu.HBM)
def attend(mask,kv,qg):
    return pl.pallas_call(attend_kernel,
        out_shape=(pltpu.VMEM(KV,BF),pltpu.VMEM(QG,BF)),
        in_specs=[ANY,VM,VM],
        out_specs=(VM,VM),
        scratch_shapes=[
            pltpu.VMEM((3*NB,BLK,TQ),BF),pltpu.VMEM((3*NB,1,TQ),F32),pltpu.VMEM((NB*BLK,HD),F32),pltpu.VMEM((NB*BLK,HD),F32),
            pltpu.VMEM((3,HD,TQ),F32),pltpu.VMEM((3,HD,TQ),F32),pltpu.VMEM((2,BLK,TQ),F32),pltpu.VMEM((3,HD,TQ),BF),pltpu.VMEM((3,HD,TQ),BF),pltpu.VMEM((3,3,1,TQ),F32),pltpu.SMEM((3*NB+1,),jnp.int32),pltpu.SMEM((3*NB+1,),jnp.int32),pltpu.SMEM((NB,NB),jnp.int32),DMA((1,))],
        name="attend",
        compiler_params=pltpu.CompilerParams(vmem_limit_bytes=40<<20))(afar(mask),held(kv),held(qg))

MESH=pl.DeviceIdType.MESH

def place():
    ctx=lax.axis_index("ctx"); hd=lax.axis_index("head")
    return ctx//8, ctx%8, hd//8, (hd%8)//2, hd%2

def device(x, z, y, c):
    return ((x%2)*8+z, (x//2)*8+y*2+c)

def owner(tile):
    blk=tile//2; t=blk//4
    return chip_of(blk), (tile%2+t)%2, t

def order(i):
    return (i%2)*((i+1)//2)+(1-i%2)*((8-i//2)%8)

def remote(src, dst, send, recv, dev):
    return pltpu.make_async_remote_copy(src_ref=src, dst_ref=dst, send_sem=send, recv_sem=recv,
                                        device_id=dev, device_id_type=MESH)

def wait_for(ref, sem):
    pltpu.make_async_copy(ref,ref,sem).wait()

def greet(x, z, y, c):
    barrier=pltpu.get_barrier_semaphore()
    def plane(i,_):
        s=(z*4+y+i)%32
        pl.semaphore_signal(barrier, inc=1, device_id=device(x,s//4,s%4,c), device_id_type=MESH)
        return 0
    lax.fori_loop(1,32,plane,0,unroll=True)
    for i in range(1,8):
        s=(x*2+c+i)%8
        pl.semaphore_signal(barrier, inc=1, device_id=device(s//2,z,y,s%2), device_id_type=MESH)

def greeted():
    pl.semaphore_wait(pltpu.get_barrier_semaphore(), 38)

def gather_kernel(off_hbm, q, k, v, g, kv, qg, q_vm, k_vm, v_vm, g_vm, kv_out, qg_out, qg_in,
                  off, ld, a_send, a_recv, b_send, b_recv, x_send, x_recv, f_send, f_recv, c_send, c_recv, o_send, o_recv):
    x_lo,z,x_hi,y,c=place()
    x=x_hi*2+x_lo
    right=(x+1)%4; left=(x+3)%4; far=(x+2)%4
    mine=z*4+y
    greet(x,z,y,c)
    for i in range(8):
        cols=pl.ds(pl.multiple_of(((z+order(i))%8)*512,512),512)
        pltpu.make_async_copy(k.at[:,:,cols],k_vm.at[:,:,cols],ld.at[i]).start()
        pltpu.make_async_copy(v.at[:,:,cols],v_vm.at[:,:,cols],ld.at[i]).start()
    pltpu.make_async_copy(q,q_vm,ld.at[8]).start()
    pltpu.make_async_copy(g,g_vm,ld.at[9]).start()
    fetch=pltpu.make_async_copy(off_hbm,off,ld.at[10])
    fetch.start()
    row=lax.broadcasted_iota(jnp.int32,(24,96),0); col=lax.broadcasted_iota(jnp.int32,(24,96),1)
    lead=col-row*4
    def columns(h):
        return pl.ds(pl.multiple_of(h*HD,HD),HD)
    def pick(ref,h,hot):
        return dot(hot,ref[:,:,columns(h)].reshape(96,HD)).reshape(3,8,HD).astype(BF)
    def hot_of(h):
        return (lead==off[h]).astype(F32).astype(BF)
    def chunk(x2,z2):
        return kv.at[:,x2%2,z2,x2//2,:,c]
    def pick_kv(i):
        wait_for(k_vm.at[:,:,pl.ds(0,1024)],ld.at[i])
        z2=(z+order(i))%8
        for j in range(4):
            h=z2*4+(y+j)%4
            hot=hot_of(h)
            kv_out[h,0]=pick(k_vm,h,hot)
            kv_out[h,1]=pick(v_vm,h,hot)
    def pick_qg(i):
        z2=(z+order(i))%8
        for j in range(4):
            h=z2*4+(y+j)%4
            qg_out[h,0]=pick(q_vm,h,hot_of(h))
            qg_out[h,1]=g_vm[:,:,columns(h)]
    def to_plane(i, out, dst, send, recv):
        z2=(z+order(i))%8
        for j in range(4):
            y2=(y+j)%4
            src=out.at[z2*4+y2]
            if j:
                remote(src,dst,send,recv,device(x,z2,y2,c)).start()
            else:
                @pl.when(z2!=z)
                def _():
                    remote(src,dst,send,recv,device(x,z2,y2,c)).start()
                @pl.when(z2==z)
                def _():
                    pltpu.make_async_copy(src,dst,recv).start()
    def send_kv(i):
        to_plane(i,kv_out,kv.at[:,x_lo,z,x_hi,y,c],a_send.at[0],a_recv.at[i])
    def send_qg(i):
        to_plane(i,qg_out,qg_in.at[mine],b_send.at[0],b_recv.at[i])
    def ring(i):
        z2=(z+8-order(i))%8
        wait_for(kv_out.at[0:4],a_recv.at[i])
        own=chunk(x,z2)
        remote(own,own,x_send.at[0],x_recv.at[0,i],device(right,z,y,c)).start()
        remote(own,own,x_send.at[1],x_recv.at[1,i],device(left,z,y,c)).start()
        remote(own,own,c_send.at[0],c_recv.at[0],device(x,z,y,1-c)).start()
    def halves(i):
        z2=(z+8-order(i))%8
        for d,frm,to in ((0,left,right),(1,right,left)):
            a=chunk(frm,z2)
            wait_for(a,x_recv.at[d,i])
            ah=a.at[:,2*d:2*d+2]
            remote(ah,ah,f_send.at[d],f_recv.at[i],device(to,z,y,c)).start()
            remote(a,a,c_send.at[0],c_recv.at[0],device(x,z,y,1-c)).start()
    def last(i):
        z2=(z+8-order(i))%8
        a=chunk(far,z2)
        wait_for(a,f_recv.at[i])
        remote(a,a,c_send.at[0],c_recv.at[0],device(x,z,y,1-c)).start()
    def hand(s,first,count,unit,op):
        tile=unit//32; u=unit%32
        xo,co,t=owner(tile)
        src=qg_in.at[s,:,pl.ds(first,count)]; dst=qg.at[t,:,pl.ds(u,count)]
        @pl.when((xo!=x)|(co!=c))
        def _():
            cp=remote(src,dst,o_send.at[0],o_recv.at[0],device(xo,z,y,co))
            if op=="start": cp.start()
            else: cp.wait_send()
        if op=="start":
            @pl.when((xo==x)&(co==c))
            def _():
                pltpu.make_async_copy(src,dst,o_recv.at[0]).start()
    def spread(i,op):
        z2=(z+8-order(i))%8
        if op=="start":
            wait_for(qg_in.at[0:4],b_recv.at[i])
        def one(y2,_):
            s=z2*4+y2
            unit=(((x_lo*8+z2)*2+x_hi)*8+y2*2+c)*3
            @pl.when((unit%32)<=29)
            def _():
                hand(s,0,3,unit,op)
            @pl.when((unit%32)>29)
            def _():
                for e in range(3):
                    hand(s,e,1,unit+e,op)
            return 0
        lax.fori_loop(0,4,one,0)
    def loop(lo,hi,*acts):
        def body(i,_):
            for act in acts: act(i)
            return 0
        lax.fori_loop(lo,hi,body,0)
    def seq(lo,hi,*acts):
        loop(lo,hi,*[(lambda i,f=f,d=d: f(i+d)) for f,d in acts])
    def spread_start(i):
        spread(i,"start")
    fetch.wait()
    pick_kv(0)
    greeted()
    send_kv(0)
    loop(1,8,pick_kv,send_kv)
    wait_for(q_vm,ld.at[8]); wait_for(g_vm,ld.at[9])
    loop(0,8,pick_qg,send_qg)
    loop(0,4,ring)
    seq(4,8,(ring,0),(halves,-4))
    seq(4,8,(halves,0),(spread_start,-4))
    seq(0,4,(last,0),(spread_start,4))
    loop(4,8,last)
    wait_for(kv_out.at[0:31],a_send.at[0])
    wait_for(qg_out.at[0:31],b_send.at[0])
    loop(0,8,lambda i: spread(i,"done"))
    for d in range(2):
        wait_for(kv.at[:,0,:,0,:,0],x_send.at[d])
        wait_for(kv.at[:,0,:,0,0:2,0],f_send.at[d])
    wait_for(kv.at[:,:,:,:,:,0],c_send.at[0])
    wait_for(kv.at[:,:,:,:,:,0],c_recv.at[0])
    wait_for(qg,o_recv.at[0])

def gather(off,q,k,v,g):
    return pl.pallas_call(gather_kernel,
        out_shape=(pltpu.VMEM(KV,BF),pltpu.VMEM(QG,BF)),
        in_specs=[ANY]*5,
        out_specs=(VM,VM),
        scratch_shapes=[pltpu.VMEM((24,4,4096),BF)]*3+[pltpu.VMEM((3,8,4096),BF)]+[pltpu.VMEM((32,2,3,8,HD),BF)]*3+[
            pltpu.SMEM((HEADS,),jnp.int32),DMA((11,)),DMA((1,)),DMA((8,)),DMA((1,)),DMA((8,)),DMA((2,)),DMA((2,8)),DMA((2,)),DMA((8,)),DMA((1,)),DMA((1,)),DMA((1,)),DMA((1,))],
        name="gather",
        compiler_params=pltpu.CompilerParams(collective_id=0,has_side_effects=True,vmem_limit_bytes=40<<20))(*[afar(a) for a in (off,q,k,v,g)])

def scatter_kernel(dkv, og, out,
                   own, far_in, near_in, last_in, og_in, fin,
                   c_send, c_recv, g_send, g_recv, far_send, far_recv, near_send, last_send, fin_recv, p_send, p_recv):
    x_lo,z,x_hi,y,c=place()
    x=x_hi*2+x_lo
    right=(x+1)%4; left=(x+3)%4; far=(x+2)%4
    mine=z*4+y
    cols=pl.ds(pl.multiple_of(mine*HD,HD),HD)
    def at_z(i):
        return (z+order(7-i))%8
    greet(x,z,y,c)
    greeted()
    def back(op):
        def one(i,_):
            t=i//12; e=i%12
            blk=block_of(x,t)
            tile=2*blk+(c+t)%2
            def hand(unit,count):
                piece=unit//3; k=unit%3; u=unit-tile*32
                xp=((piece//8)%2)*2+(piece//128)
                zp=(piece//16)%8; yp=(piece%8)//2; cp_=piece%2
                s=zp*4+yp
                src=og.at[t,:,pl.ds(u,count)]; dst=og_in.at[s,:,pl.ds(k,count)]
                sem=g_recv.at[zp]
                @pl.when((xp!=x)|(cp_!=c))
                def _():
                    cp=remote(src,dst,g_send.at[0],sem,device(xp,z,y,cp_))
                    if op=="start": cp.start()
                    else: cp.wait_send()
                if op=="start":
                    @pl.when((xp==x)&(cp_==c))
                    def _():
                        pltpu.make_async_copy(src,dst,sem).start()
            @pl.when(e<10)
            def _():
                hand(((tile*32+2)//3+e)*3,3)
            @pl.when(e>=10)
            def _():
                n=e-10; r=tile%3
                hand(tile*32+n+30*(1-(r+1)//2)+30*n*(r%2),1)
            return 0
        lax.fori_loop(0,36,one,0)
    for i in range(8):
        z2=at_z(i)
        remote(dkv.at[:,:,z2,:,:,1-c],own.at[:,:,z2],c_send.at[0],c_recv.at[i],device(x,z,y,1-c)).start()
    back("start")
    def to_rows(a, src, s, j):
        dst=out.at[2*a:2*a+2,:,:,cols]
        def away():
            remote(src,dst,p_send.at[a],p_recv.at[a],device(x,s//4,s%4,c)).start()
        if j:
            away()
        else:
            pl.when(s!=mine)(away)
            @pl.when(s==mine)
            def _():
                pltpu.make_async_copy(src,dst,p_recv.at[a]).start()
    def sum_cores(i):
        z2=at_z(i)
        wait_for(own.at[:,:,z2],c_recv.at[i])
        for xl in range(2):
            for xh in range(2):
                own[:,xl,z2,xh]=(own[:,xl,z2,xh].astype(F32)+dkv[:,xl,z2,xh,:,c].astype(F32)).astype(BF)
        ef=own.at[:,far%2,z2,far//2]
        remote(ef.at[:,0:2],far_in.at[0,z2],far_send.at[0],far_recv.at[0,i],device(right,z,y,c)).start()
        remote(ef.at[:,2:4],far_in.at[1,z2],far_send.at[0],far_recv.at[1,i],device(left,z,y,c)).start()
    def rows_back(i):
        z2=at_z(i)
        wait_for(og_in.at[0:4],g_recv.at[z2])
        for j in range(4):
            s=z2*4+(y+j)%4
            to_rows(0,og_in.at[s],s,j)
    def relay(i):
        z2=at_z(i)
        for d,peer in ((0,right),(1,left)):
            lo=2*d
            buf=far_in.at[d,z2]
            wait_for(buf,far_recv.at[d,i])
            far_in[d,z2]=(far_in[d,z2].astype(F32)+own[:,peer%2,z2,peer//2,lo:lo+2].astype(F32)).astype(BF)
            remote(buf,last_in.at[d,z2],last_send.at[0],fin_recv.at[i],device(peer,z,y,c)).start()
        er=own.at[:,right%2,z2,right//2]; el=own.at[:,left%2,z2,left//2]
        remote(er.at[:,2:4],near_in.at[0,z2],near_send.at[0],fin_recv.at[i],device(right,z,y,c)).start()
        remote(el.at[:,0:2],near_in.at[1,z2],near_send.at[0],fin_recv.at[i],device(left,z,y,c)).start()
    def finish(i):
        z2=at_z(i)
        wait_for(own.at[:,0,z2],fin_recv.at[i])
        for d in range(2):
            lo=2*d
            fin[:,pl.ds(z2*4+lo,2)]=(own[:,x_lo,z2,x_hi,lo:lo+2].astype(F32)+last_in[d,z2].astype(F32)+near_in[1-d,z2].astype(F32)).astype(BF)
        for j in range(4):
            s=z2*4+(y+j)%4
            to_rows(1,fin.at[:,s],s,j)
    def loop(lo,hi,*acts):
        def body(i,_):
            for act in acts: act(i)
            return 0
        lax.fori_loop(lo,hi,body,0)
    loop(0,8,sum_cores)
    loop(0,2,rows_back)
    loop(0,6,relay,lambda i: rows_back(i+2))
    loop(6,8,relay)
    loop(0,8,finish)
    back("done")
    wait_for(own,c_send.at[0])
    for b,sem in ((far_in,far_send),(near_in,near_send),(last_in,last_send)):
        wait_for(b,sem.at[0])
    wait_for(og_in.at[0:31],p_send.at[0])
    wait_for(fin.at[:,0:31],p_send.at[1])
    for a in range(2):
        wait_for(out.at[2*a:2*a+2],p_recv.at[a])

def scatter(dkv,og):
    return pl.pallas_call(scatter_kernel,
        out_shape=pltpu.VMEM((4,3,8,4096),BF),
        in_specs=[VM]*2,
        out_specs=VM,
        scratch_shapes=[pltpu.VMEM((2,2,8,2,4,3,8,HD),BF)]+[pltpu.VMEM((2,8,2,2,3,8,HD),BF)]*3+[pltpu.VMEM((32,2,3,8,HD),BF),pltpu.VMEM((2,32,3,8,HD),BF),
            DMA((1,)),DMA((8,)),DMA((1,)),DMA((8,)),DMA((1,)),DMA((2,8)),DMA((1,)),DMA((1,)),DMA((8,)),DMA((2,)),DMA((2,))],
        name="scatter",
        compiler_params=pltpu.CompilerParams(collective_id=1,has_side_effects=True,vmem_limit_bytes=40<<20))(held(dkv),held(og))

def settle_kernel(src,*refs):
    cps=[pltpu.make_async_copy(src.at[i],refs[i],refs[4].at[i]) for i in range(4)]
    for cp in cps: cp.start()
    for cp in cps: cp.wait()

def settle(out):
    return pl.pallas_call(settle_kernel,
        out_shape=(jax.ShapeDtypeStruct((3,8,4096),BF),)*4,
        in_specs=[VM],out_specs=(ANY,)*4,
        scratch_shapes=[DMA((4,))],
        name="settle",
        compiler_params=pltpu.CompilerParams(vmem_limit_bytes=40<<20))(held(out))

def on_device(queries,key_states,value_states,out_grad,offsets,block_mask):
    kv,qg=gather(offsets,queries,key_states,value_states,out_grad.reshape(3,8,4096))
    dkv,og=attend(block_mask,kv,qg)
    outs=settle(scatter(dkv,og))
    return tuple(o.reshape(24,4096) for o in outs)


def solution(mesh):
    rows3=P(("ctx","head"),None,None); rows2=P(("ctx","head"),None)
    return jax.shard_map(on_device,mesh=mesh,in_specs=(rows3,rows3,rows3,rows2,P(),P()),
                         out_specs=(rows2,)*4,check_vma=False)
```
